32 devices in a mesh: ctx: 8 (over y, x, core), roll: 4 (over z).
Axes of the slice: x: 2, y: 2, z: 4, core: 2. Of those that a mesh axis runs over, the one named last changes fastest.
Arguments:
- prompt_query: bfloat16 [1024, 8192], P('ctx', 'roll'), may hold values from -3 to 3
- prompt_key_rows: bfloat16 [1024, 1024], P('ctx', 'roll'), may hold values from -3 to 3
- prompt_value_rows: bfloat16 [1024, 1024], P('ctx', 'roll'), may hold values from -4 to 4
- prompt_dout: bfloat16 [1024, 8192], P('ctx', 'roll'), may hold values from -72 to 72
- prompt_out: bfloat16 [1024, 8192], P('ctx', 'roll'), may hold values from -3 to 3
- prompt_lse: bfloat16 [1024, 64], P('ctx', 'roll'), may hold values from 7.5 to 9.5
- roll_query: bfloat16 [1024, 8192], P(('ctx', 'roll')), may hold values from -3 to 3
- rollout_key_rows: bfloat16 [1024, 1024], P(('ctx', 'roll')), may hold values from -3 to 3
- rollout_value_rows: bfloat16 [1024, 1024], P(('ctx', 'roll')), may hold values from -4 to 4
- roll_dout: bfloat16 [1024, 8192], P(('ctx', 'roll')), may hold values from -72 to 72
- roll_out: bfloat16 [1024, 8192], P(('ctx', 'roll')), may hold values from -3 to 3
- roll_lse: bfloat16 [1024, 64], P(('ctx', 'roll')), may hold values from 7.5 to 9.5
Outputs:
- prompt_dq: bfloat16 [1024, 8192], P('ctx', 'roll')
- prompt_dk: bfloat16 [1024, 1024], P('ctx', 'roll')
- prompt_dv: bfloat16 [1024, 1024], P('ctx', 'roll')
- roll_dq: bfloat16 [1024, 8192], P(('ctx', 'roll'))
- roll_dk: bfloat16 [1024, 1024], P(('ctx', 'roll'))
- roll_dv: bfloat16 [1024, 1024], P(('ctx', 'roll'))
The draws below stay inside these ranges and needn't reach their ends.
All inputs are finite; a program needn't handle non-finite values.
Results may differ from the reference program's by a relative error of at most 0.0095.
Values may be sent and summed in bfloat16 or wider, within the bound.
No kernel may reach another device: no remote copies, remote signals or barrier semaphores. Data moves between devices by JAX's collectives and lax.ppermute only.
A program may use at most 64 MiB of HBM per device.

```python
import math
import jax
import jax.numpy as jnp
from jax import lax

QUERY_HEAD_COUNT = 64
KV_HEAD_COUNT = 8
HEAD_SIZE = 128
PT = 128
LEN = 128
PROMPT_TOKENS = 1024
ROLLOUT_TOKENS = 1024
N_CTX = 8


def level_of(stream_key, extent, split, low, high):
    gain = 1.0
    for axis_at, blocks in split:
        draws = jax.random.uniform(jax.random.fold_in(jax.random.fold_in(stream_key, 6), axis_at), (blocks,), jnp.float32, low / len(split), high / len(split))
        gain = gain * jnp.repeat(jnp.exp(draws), extent[axis_at] // blocks).reshape((-1,) + (1,) * (len(extent) - 1 - axis_at))
    return gain


def gaussian(own_key, extent, deviation, most, cuts=(), kind=jnp.bfloat16):
    factor_of = level_of(own_key, extent, cuts, -0.22, 0.18) if cuts else 1.0
    values = jax.random.normal(own_key, extent, jnp.float32) * deviation * factor_of
    return jnp.minimum(jnp.maximum(values, -most), most).astype(kind)


def setup_inputs(seed: int = 0) -> dict:
    streams_of = jax.random.split(jax.random.key(seed), 13)
    return {
        "prompt_query": gaussian(streams_of[0], (PROMPT_TOKENS, QUERY_HEAD_COUNT * HEAD_SIZE), 1.0, 3.0, ((0, 8), (1, 4))),
        "prompt_key_rows": gaussian(streams_of[1], (PROMPT_TOKENS, KV_HEAD_COUNT * HEAD_SIZE), 1.0, 3.0, ((0, 8), (1, 4))),
        "prompt_value_rows": gaussian(streams_of[2], (PROMPT_TOKENS, KV_HEAD_COUNT * HEAD_SIZE), 1.0, 4.0, ((0, 8), (1, 4))),
        "prompt_dout": gaussian(streams_of[3], (PROMPT_TOKENS, QUERY_HEAD_COUNT * HEAD_SIZE), 12.0, 72.0, ((0, 8), (1, 4))),
        "prompt_out": gaussian(streams_of[4], (PROMPT_TOKENS, QUERY_HEAD_COUNT * HEAD_SIZE), 0.5, 3.0, ((0, 8), (1, 4))),
        "prompt_lse": jnp.clip(7.5 + 2.0 * jax.random.uniform(streams_of[5], (PROMPT_TOKENS, QUERY_HEAD_COUNT), jnp.float32) ** level_of(streams_of[5], (PROMPT_TOKENS, QUERY_HEAD_COUNT), ((0, 8), (1, 4)), -0.2, 0.2), 7.5, 9.5).astype(jnp.bfloat16),
        "roll_query": gaussian(streams_of[6], (ROLLOUT_TOKENS, QUERY_HEAD_COUNT * HEAD_SIZE), 1.0, 3.0, ((0, 32),)),
        "rollout_key_rows": gaussian(streams_of[7], (ROLLOUT_TOKENS, KV_HEAD_COUNT * HEAD_SIZE), 1.0, 3.0, ((0, 32),)),
        "rollout_value_rows": gaussian(streams_of[8], (ROLLOUT_TOKENS, KV_HEAD_COUNT * HEAD_SIZE), 1.0, 4.0, ((0, 32),)),
        "roll_dout": gaussian(streams_of[9], (ROLLOUT_TOKENS, QUERY_HEAD_COUNT * HEAD_SIZE), 12.0, 72.0, ((0, 32),)),
        "roll_out": gaussian(streams_of[10], (ROLLOUT_TOKENS, QUERY_HEAD_COUNT * HEAD_SIZE), 0.5, 3.0, ((0, 32),)),
        "roll_lse": jnp.clip(7.5 + 2.0 * jax.random.uniform(streams_of[11], (ROLLOUT_TOKENS, QUERY_HEAD_COUNT), jnp.float32) ** level_of(streams_of[11], (ROLLOUT_TOKENS, QUERY_HEAD_COUNT), ((0, 32),), -0.2, 0.2), 7.5, 9.5).astype(jnp.bfloat16),
    }


def positions(row_ids, half_rows, cycle_count):
    block_index = row_ids // half_rows
    pair_index = block_index // 2
    offset = row_ids % half_rows
    return jnp.where(block_index % 2 == 0, pair_index * half_rows + offset, (2 * cycle_count - 1 - pair_index) * half_rows + offset).astype(jnp.int32)

def head_sums(grad_out, outputs):
    product = grad_out.astype(jnp.float32) * outputs.astype(jnp.float32)
    return product.reshape(product.shape[0], -1, HEAD_SIZE).sum(axis=2)

def rounded(tensor):
    return lax.optimization_barrier(tensor.astype(jnp.bfloat16)).astype(jnp.float32)

def tile_grads(queries, grad_out, log_sums, delta_sums, query_pos, key_tile, value_tile, key_pos):
    query_rows = queries.shape[0]
    key_rows = key_tile.shape[0]
    groups = key_tile.shape[1] // HEAD_SIZE
    group_members = queries.shape[1] // (groups * HEAD_SIZE)
    scaling = 1.0 / math.sqrt(HEAD_SIZE)
    query_heads = queries.astype(jnp.float32).reshape(query_rows, groups, group_members, HEAD_SIZE)
    grad_heads = grad_out.astype(jnp.float32).reshape(query_rows, groups, group_members, HEAD_SIZE)
    key_heads = key_tile.astype(jnp.float32).reshape(key_rows, groups, HEAD_SIZE)
    value_heads = value_tile.astype(jnp.float32).reshape(key_rows, groups, HEAD_SIZE)
    scores = jnp.einsum('qgmd,kgd->gmqk', query_heads, key_heads) * scaling
    lse_cols = log_sums.astype(jnp.float32).reshape(query_rows, groups, group_members).transpose(1, 2, 0)[..., None]
    delta_cols = delta_sums.reshape(query_rows, groups, group_members).transpose(1, 2, 0)[..., None]
    allowed = key_pos[None, :] <= query_pos[:, None]
    probs = jnp.where(allowed, jnp.exp(scores - lse_cols), 0.0)
    grad_probs = jnp.einsum('qgmd,kgd->gmqk', grad_heads, value_heads)
    grad_scores = rounded(probs * (grad_probs - delta_cols))
    probs_low = rounded(probs)
    grad_query = jnp.einsum('gmqk,kgd->qgmd', grad_scores, key_heads).reshape(query_rows, -1) * scaling
    grad_key = jnp.einsum('gmqk,qgmd->kgd', grad_scores, query_heads).reshape(key_rows, -1) * scaling
    grad_value = jnp.einsum('gmqk,qgmd->kgd', probs_low, grad_heads).reshape(key_rows, -1)
    return (grad_query, grad_key, grad_value)

def reference(prompt_query, prompt_key_rows, prompt_value_rows, prompt_dout, prompt_out, prompt_lse, roll_query, rollout_key_rows, rollout_value_rows, roll_dout, roll_out, roll_lse):
    prompt_rows = PT * N_CTX
    roll_rows = LEN * N_CTX
    prompt_pos = positions(jnp.arange(prompt_rows, dtype=jnp.int32), PT // 2, N_CTX)
    queries = jnp.concatenate([prompt_query, roll_query], 0)
    grad_out = jnp.concatenate([prompt_dout, roll_dout], 0)
    log_sums = jnp.concatenate([prompt_lse, roll_lse], 0)
    delta_sums = head_sums(grad_out, jnp.concatenate([prompt_out, roll_out], 0))
    query_pos = jnp.concatenate([prompt_pos, jnp.full((roll_rows,), prompt_rows, jnp.int32)])
    group_members = QUERY_HEAD_COUNT // KV_HEAD_COUNT
    key_block = math.gcd(prompt_rows, 512)
    key_pos = prompt_pos.reshape(-1, key_block)
    query_parts, key_parts, value_parts = ([], [], [])
    for shared_head_group in range(KV_HEAD_COUNT):
        low_col = shared_head_group * group_members * HEAD_SIZE
        high_col = low_col + group_members * HEAD_SIZE
        group_queries = queries[:, low_col:high_col]
        group_grads = grad_out[:, low_col:high_col]
        group_lse = log_sums[:, shared_head_group * group_members:(shared_head_group + 1) * group_members]
        group_delta = delta_sums[:, shared_head_group * group_members:(shared_head_group + 1) * group_members]
        group_keys = prompt_key_rows[:, shared_head_group * HEAD_SIZE:(shared_head_group + 1) * HEAD_SIZE].reshape(-1, key_block, HEAD_SIZE)
        group_values = prompt_value_rows[:, shared_head_group * HEAD_SIZE:(shared_head_group + 1) * HEAD_SIZE].reshape(-1, key_block, HEAD_SIZE)

        def key_step(running, pieces):
            grad_query, grad_key, grad_value = tile_grads(group_queries, group_grads, group_lse, group_delta, query_pos, pieces[0], pieces[1], pieces[2])
            return (running + grad_query, (grad_key, grad_value))
        start_zero = jnp.zeros((queries.shape[0], group_members * HEAD_SIZE), jnp.float32)
        running, (grad_key, grad_value) = lax.scan(key_step, start_zero, (group_keys, group_values, key_pos))
        query_parts.append(running)
        key_parts.append(grad_key.reshape(prompt_rows, HEAD_SIZE))
        value_parts.append(grad_value.reshape(prompt_rows, HEAD_SIZE))
    query_grads = jnp.concatenate(query_parts, 1)

    def suffix(pieces):
        places = jnp.arange(LEN, dtype=jnp.int32)
        return tile_grads(pieces[0], pieces[3], pieces[4], pieces[5], places, pieces[1], pieces[2], places)
    roll_delta = delta_sums[prompt_rows:].reshape(N_CTX, LEN, -1)
    own_query, roll_keygrad, roll_valgrad = lax.map(suffix, (roll_query.reshape(N_CTX, LEN, -1), rollout_key_rows.reshape(N_CTX, LEN, -1), rollout_value_rows.reshape(N_CTX, LEN, -1), roll_dout.reshape(N_CTX, LEN, -1), roll_lse.reshape(N_CTX, LEN, -1), roll_delta))
    roll_total = query_grads[prompt_rows:] + own_query.reshape(roll_rows, -1)
    return (query_grads[:prompt_rows].astype(jnp.bfloat16), jnp.concatenate(key_parts, 1).astype(jnp.bfloat16), jnp.concatenate(value_parts, 1).astype(jnp.bfloat16), roll_total.astype(jnp.bfloat16), roll_keygrad.reshape(roll_rows, -1).astype(jnp.bfloat16), roll_valgrad.reshape(roll_rows, -1).astype(jnp.bfloat16))
```

```python
import functools
import math

import jax
import jax.numpy as jnp
from jax import lax
from jax.experimental import pallas as pl
from jax.experimental.pallas import tpu as pltpu
from jax.sharding import PartitionSpec as P

HEAD = 128
LOG2E = math.log2(math.e)
SCALE = 1.0 / math.sqrt(HEAD)
VMEM_LIMIT = 56 * 1024 * 1024
KEY_CHUNK = 512
ROW_CHUNK = 512

BF = jnp.bfloat16
F32 = jnp.float32


def dot_nt(a, b):
    return lax.dot_general(a, b, (((1,), (1,)), ((), ())), preferred_element_type=F32)


def dot_nn(a, b):
    return lax.dot_general(a, b, (((1,), (0,)), ((), ())), preferred_element_type=F32)


def dot_tn(a, b):
    return lax.dot_general(a, b, (((0,), (0,)), ((), ())), preferred_element_type=F32)


def split_sum(product):
    high = product.astype(BF)
    low = (product - high.astype(F32)).astype(BF)
    return high, low


def tile_grads(keys, values, queries, grads, lse_row, delta_row, mask):
    scores = dot_nt(keys, queries)
    probs = jnp.exp2(scores * (SCALE * LOG2E) - lse_row)
    if mask is not None:
        probs = jnp.where(mask, probs, 0.0)
    grad_probs = dot_nt(values, grads)
    grad_scores = (probs * (grad_probs - delta_row)).astype(BF)
    grad_value = dot_nn(probs.astype(BF), grads)
    grad_key = dot_nn(grad_scores, queries)
    grad_query = dot_tn(grad_scores, keys)
    return grad_query, grad_key, grad_value


def stacked_heads(ref, low, high, base, group, members):
    first = base + group * members * HEAD
    return jnp.concatenate(
        [ref[low:high, first + h * HEAD : first + (h + 1) * HEAD] for h in range(members)], axis=0
    )


def pack_kernel(me_ref, q_ref, do_ref, o_ref, k_ref, v_ref, lse_ref, *outs):
    parts = len(outs)
    width = q_ref.shape[1] // parts
    narrow = k_ref.shape[1] // parts
    heads = width // HEAD
    rows = q_ref.shape[0]
    me = me_ref[0]
    column = lax.broadcasted_iota(jnp.int32, (width, HEAD), 0) // HEAD
    lane = lax.broadcasted_iota(jnp.int32, (width, HEAD), 1)
    pick = jnp.where((lane == column + heads) | (lane == column + 2 * heads), 1.0, 0.0).astype(BF)
    all_heads = lse_ref.shape[1]
    lse_column = lax.broadcasted_iota(jnp.int32, (all_heads, HEAD), 0)
    lse_lane = lax.broadcasted_iota(jnp.int32, (all_heads, HEAD), 1)
    out_lane = lax.broadcasted_iota(jnp.int32, (rows, HEAD), 1)
    for k, out in enumerate(outs):
        dest = me ^ k
        wide = pl.ds(pl.multiple_of(dest * width, HEAD), width)
        thin = pl.ds(pl.multiple_of(dest * narrow, HEAD), narrow)
        grads = do_ref[:, wide]
        out[:, :width] = q_ref[:, wide]
        out[:, width : 2 * width] = grads
        out[:, 2 * width : 2 * width + narrow] = k_ref[:, thin]
        out[:, 2 * width + narrow : 2 * width + 2 * narrow] = v_ref[:, thin]
        high, low = split_sum(grads.astype(F32) * o_ref[:, wide].astype(F32))
        delta = dot_nn(high, pick) + dot_nn(low, pick)
        lse_pick = jnp.where(
            (lse_column == lse_lane + dest * heads) & (lse_lane < heads), 1.0, 0.0
        ).astype(BF)
        lse = dot_nn(lse_ref[...], lse_pick)
        delta_high = delta.astype(BF).astype(F32)
        stats = jnp.where(
            out_lane < heads, lse, jnp.where(out_lane < 2 * heads, delta_high, delta - delta_high)
        )
        out[:, 2 * width + 2 * narrow :] = stats.astype(BF)


def prompt_kernel(members, me_ref, q_ref, do_ref, o_ref, lse_ref, *rest):
    kv_refs, (dq_ref, part_ref) = rest[:-2], rest[-2:]
    slots = len(kv_refs)
    rows = q_ref.shape[0]
    half = rows // 2
    narrow = kv_refs[0].shape[1] // 2
    groups = narrow // HEAD
    me = me_ref[0]
    count = members * half
    ones = jnp.ones((8, HEAD), BF)
    chunk_slots = max(1, min(slots, KEY_CHUNK // half))
    chunk = chunk_slots * half
    key_row = lax.broadcasted_iota(jnp.int32, (chunk, 1), 0)
    query_row = lax.broadcasted_iota(jnp.int32, (1, count), 1) % half
    stat_lane = lax.broadcasted_iota(jnp.int32, (half, HEAD), 1)
    for g in range(groups):
        queries, grads, lse_rows, delta_rows = [], [], [], []
        for s in range(2):
            low, high = s * half, (s + 1) * half
            queries.append(stacked_heads(q_ref, low, high, 0, g, members))
            grads.append(stacked_heads(do_ref, low, high, 0, g, members))
            outs = stacked_heads(o_ref, low, high, 0, g, members)
            up, down = split_sum(grads[s].astype(F32) * outs.astype(F32))
            delta_rows.append((dot_nt(ones, up) + dot_nt(ones, down))[0:1])
            lse = lse_ref[low:high, :]
            picked = jnp.concatenate(
                [jnp.where(stat_lane == g * members + h, lse, jnp.zeros_like(lse)) for h in range(members)],
                axis=0,
            )
            lse_rows.append(dot_nt(ones, picked)[0:1] * LOG2E)
        grad_queries = [None, None]
        for side in range(2):
            for c in range(slots // chunk_slots):
                owned = kv_refs[c * chunk_slots : (c + 1) * chunk_slots]
                span = slice(side * half, (side + 1) * half)
                keys = jnp.concatenate([r[span, g * HEAD : (g + 1) * HEAD] for r in owned], axis=0)
                values = jnp.concatenate(
                    [r[span, narrow + g * HEAD : narrow + (g + 1) * HEAD] for r in owned], axis=0
                )
                owner = me ^ (c * chunk_slots + key_row // half)
                offset = key_row % half
                grad_key = grad_value = None
                for s in (1, 0) if side == 0 else (1,):
                    mask = None
                    if s == side:
                        ahead = owner - me if side == 0 else me - owner
                        mask = ahead * half + offset <= query_row
                    dq, dk, dv = tile_grads(
                        keys, values, queries[s], grads[s], lse_rows[s], delta_rows[s], mask
                    )
                    grad_queries[s] = dq if grad_queries[s] is None else grad_queries[s] + dq
                    grad_key = dk if grad_key is None else grad_key + dk
                    grad_value = dv if grad_value is None else grad_value + dv
                grad_key = grad_key * SCALE
                for t in range(chunk_slots):
                    piece = slice(t * half, (t + 1) * half)
                    slot = c * chunk_slots + t
                    part_ref[slot, span, g * HEAD : (g + 1) * HEAD] = grad_key[piece]
                    part_ref[slot, span, narrow + g * HEAD : narrow + (g + 1) * HEAD] = grad_value[piece]
        for s in range(2):
            result = (grad_queries[s] * SCALE).astype(BF)
            for h in range(members):
                first = (g * members + h) * HEAD
                dq_ref[s * half : (s + 1) * half, first : first + HEAD] = result[h * half : (h + 1) * half]


def roll_kernel(parts, slots, members, me_ref, *rest):
    packs, rest = rest[:parts], rest[parts:]
    kv_refs, rest = rest[:slots], rest[slots:]
    part_ref, even_ref, odd_ref = rest[:3]
    backs = rest[3:]
    me = me_ref[0]
    rows = packs[0].shape[0]
    kv_rows = kv_refs[0].shape[0]
    narrow = kv_refs[0].shape[1] // 2
    groups = narrow // HEAD
    heads = groups * members
    width = heads * HEAD
    block = members * rows
    count = parts * block
    stat_row = lax.broadcasted_iota(jnp.int32, (8, HEAD), 0)
    stat_lane = lax.broadcasted_iota(jnp.int32, (8, HEAD), 1)
    pick = jnp.where(
        ((stat_row == 0) & (stat_lane < heads))
        | ((stat_row == 1) & (stat_lane >= heads) & (stat_lane < 3 * heads)),
        1.0,
        0.0,
    ).astype(BF)
    lane_head = lax.broadcasted_iota(jnp.int32, (rows, HEAD), 1) % heads
    chunk_slots = max(1, min(slots, KEY_CHUNK // kv_rows))
    row_chunk = min(count, ROW_CHUNK)
    own_key = lax.broadcasted_iota(jnp.int32, (parts * rows, 1), 0)
    own_key_pos = (me ^ (own_key // rows)) * rows + own_key % rows
    own_query = lax.broadcasted_iota(jnp.int32, (1, count), 1)
    own_query_pos = (me ^ (own_query // block)) * rows + own_query % rows
    for g in range(groups):
        queries = jnp.concatenate([stacked_heads(p, 0, rows, 0, g, members) for p in packs], axis=0)
        grads = jnp.concatenate([stacked_heads(p, 0, rows, width, g, members) for p in packs], axis=0)
        picked = []
        for p in packs:
            stats = p[:, 2 * width + 2 * narrow :]
            for h in range(members):
                picked.append(jnp.where(lane_head == g * members + h, stats, jnp.zeros_like(stats)))
        stat_rows = dot_nt(pick, jnp.concatenate(picked, axis=0))
        lse_row = stat_rows[0:1] * LOG2E
        delta_row = stat_rows[1:2]
        first = 2 * width + g * HEAD
        own_keys = jnp.concatenate([p[:, first : first + HEAD] for p in packs], axis=0)
        own_values = jnp.concatenate([p[:, first + narrow : first + narrow + HEAD] for p in packs], axis=0)
        grad_query, own_dk, own_dv = tile_grads(
            own_keys, own_values, queries, grads, lse_row, delta_row, own_key_pos <= own_query_pos
        )
        own_dk = (own_dk * SCALE).astype(BF)
        own_dv = own_dv.astype(BF)
        for k, back in enumerate(backs):
            piece = slice(k * rows, (k + 1) * rows)
            back[:, width + g * HEAD : width + (g + 1) * HEAD] = own_dk[piece]
            back[:, width + narrow + g * HEAD : width + narrow + (g + 1) * HEAD] = own_dv[piece]
        grad_rows = [grad_query[r : r + row_chunk] for r in range(0, count, row_chunk)]
        for c in range(slots // chunk_slots):
            owned = kv_refs[c * chunk_slots : (c + 1) * chunk_slots]
            keys = jnp.concatenate([r[:, g * HEAD : (g + 1) * HEAD] for r in owned], axis=0)
            values = jnp.concatenate(
                [r[:, narrow + g * HEAD : narrow + (g + 1) * HEAD] for r in owned], axis=0
            )
            grad_key = grad_value = None
            for i in range(count // row_chunk):
                piece = slice(i * row_chunk, (i + 1) * row_chunk)
                dq, dk, dv = tile_grads(
                    keys, values, queries[piece], grads[piece], lse_row[:, piece], delta_row[:, piece], None
                )
                grad_rows[i] = grad_rows[i] + dq
                grad_key = dk if grad_key is None else grad_key + dk
                grad_value = dv if grad_value is None else grad_value + dv
            grad_key = grad_key * SCALE
            for t in range(chunk_slots):
                slot = c * chunk_slots + t
                piece = slice(t * kv_rows, (t + 1) * kv_rows)
                for total, base in ((grad_key, 0), (grad_value, narrow)):
                    cols = slice(base + g * HEAD, base + (g + 1) * HEAD)
                    value = total[piece] + part_ref[slot, :, cols]
                    if slot % 2 == 0:
                        even_ref[slot // 2, :, cols] = value
                    else:
                        odd_ref[slot // 2, :, cols] = value.astype(BF)
        result = jnp.concatenate([(r * SCALE).astype(BF) for r in grad_rows], axis=0)
        for k, back in enumerate(backs):
            for h in range(members):
                start = k * block + h * rows
                first = (g * members + h) * HEAD
                back[:, first : first + HEAD] = result[start : start + rows]


def add_kernel(even_ref, got_ref, own_ref, *outs):
    own_ref[...] = even_ref[0] + got_ref[0].astype(F32)
    for t, out in enumerate(outs):
        out[...] = (even_ref[t + 1] + got_ref[t + 1].astype(F32)).astype(BF)


def final_kernel(parts, others, me_ref, own_ref, *rest):
    got, rest = rest[:others], rest[others:]
    backs, outs = rest[:parts], rest[parts:]
    pk_ref, pv_ref, rq_ref, rk_ref, rv_ref = outs
    me = me_ref[0]
    total = own_ref[...]
    for r in got:
        total = total + r[...].astype(F32)
    narrow = pk_ref.shape[1]
    pk_ref[...] = total[:, :narrow].astype(BF)
    pv_ref[...] = total[:, narrow:].astype(BF)
    width = rq_ref.shape[1] // parts
    for k, back in enumerate(backs):
        dest = me ^ k
        rq_ref[:, pl.ds(pl.multiple_of(dest * width, HEAD), width)] = back[:, :width]
        thin = pl.ds(pl.multiple_of(dest * narrow, HEAD), narrow)
        rk_ref[:, thin] = back[:, width : width + narrow]
        rv_ref[:, thin] = back[:, width + narrow :]


VMEM = pl.BlockSpec(memory_space=pltpu.VMEM)
SMEM = pl.BlockSpec(memory_space=pltpu.SMEM)


def call(kernel, name, outs, args, flops=0, scalar=True):
    moved = sum(math.prod(a.shape) * a.dtype.itemsize for a in list(args) + list(outs))
    return pl.pallas_call(
        kernel,
        name=name,
        out_shape=outs,
        in_specs=[SMEM] * scalar + [VMEM] * (len(args) - scalar),
        out_specs=[VMEM] * len(outs),
        compiler_params=pltpu.CompilerParams(vmem_limit_bytes=VMEM_LIMIT),
        cost_estimate=pl.CostEstimate(flops=flops, bytes_accessed=moved, transcendentals=0),
    )(*args)


def shape(dims, dtype):
    return jax.ShapeDtypeStruct(dims, dtype)


def swap(x, axis, k):
    n = lax.axis_size(axis)
    return lax.ppermute(x, axis, [(i, i ^ k) for i in range(n)])


def on_device(
    prompt_query,
    prompt_key_rows,
    prompt_value_rows,
    prompt_dout,
    prompt_out,
    prompt_lse,
    roll_query,
    rollout_key_rows,
    rollout_value_rows,
    roll_dout,
    roll_out,
    roll_lse,
):
    slots = lax.axis_size("ctx")
    parts = lax.axis_size("roll")
    ctx_id = lax.axis_index("ctx").astype(jnp.int32).reshape(1)
    roll_id = lax.axis_index("roll").astype(jnp.int32).reshape(1)
    prompt_rows, width = prompt_query.shape
    narrow = prompt_key_rows.shape[1]
    members = width // narrow
    heads = width // HEAD
    rows = roll_query.shape[0]
    packed = 2 * width + 2 * narrow + HEAD

    packs = call(
        pack_kernel,
        "pack",
        [shape((rows, packed), BF)] * parts,
        (roll_id, roll_query, roll_dout, roll_out, rollout_key_rows, rollout_value_rows, roll_lse),
    )
    kv = jnp.concatenate([prompt_key_rows, prompt_value_rows], axis=1)
    got = [packs[0]] + [None] * (parts - 1)
    for k in sorted(range(1, parts), key=lambda k: (k % 2 == 0, k)):
        got[k] = swap(packs[k], "roll", k)

    blocks = [None] * slots
    for s in range(0, slots, 2):
        blocks[s] = kv if s == 0 else swap(kv, "ctx", s)
    for s in range(0, slots, 2):
        blocks[s + 1] = swap(blocks[s], "ctx", 1)

    lse_padded = jnp.pad(prompt_lse, ((0, 0), (0, HEAD - heads)))
    unit = 2 * 5 * heads * HEAD * prompt_rows * slots
    prompt_dq, part = call(
        functools.partial(prompt_kernel, members),
        "prompt_grads",
        [shape((prompt_rows, width), BF), shape((slots, prompt_rows, 2 * narrow), F32)],
        (ctx_id, prompt_query, prompt_dout, prompt_out, lse_padded, *blocks),
        flops=unit * prompt_rows * 3 // 2,
    )
    even, odd, *backs = call(
        functools.partial(roll_kernel, parts, slots, members),
        "roll_grads",
        [
            shape((slots // 2, prompt_rows, 2 * narrow), F32),
            shape((slots // 2, prompt_rows, 2 * narrow), BF),
        ]
        + [shape((rows, width + 2 * narrow), BF)] * parts,
        (roll_id, *got, *blocks, part),
        flops=unit * rows * parts * 2,
    )
    returned = [backs[0]] + [None] * (parts - 1)
    for k in sorted(range(1, parts), key=lambda k: (k % 2 == 0, k)):
        returned[k] = swap(backs[k], "roll", k)
    odd_got = swap(odd, "ctx", 1)
    own, *sums = call(
        add_kernel,
        "pair_sum",
        [shape((prompt_rows, 2 * narrow), F32)] + [shape((prompt_rows, 2 * narrow), BF)] * (slots // 2 - 1),
        (even, odd_got),
        scalar=False,
    )
    sums = [swap(x, "ctx", 2 * (t + 1)) for t, x in enumerate(sums)]
    prompt_dk, prompt_dv, roll_dq, roll_dk, roll_dv = call(
        functools.partial(final_kernel, parts, len(sums)),
        "finish",
        [
            shape((prompt_rows, narrow), BF),
            shape((prompt_rows, narrow), BF),
            shape((rows, parts * width), BF),
            shape((rows, parts * narrow), BF),
            shape((rows, parts * narrow), BF),
        ],
        (roll_id, own, *sums, *returned),
    )
    return prompt_dq, prompt_dk, prompt_dv, roll_dq, roll_dk, roll_dv


def solution(mesh):
    both = P(("ctx", "roll"), None)
    split = P("ctx", "roll")
    return jax.shard_map(
        on_device,
        mesh=mesh,
        in_specs=(split,) * 6 + (both,) * 6,
        out_specs=(split,) * 3 + (both,) * 3,
        check_vma=False,
    )
```

```python
import functools
import math

import jax
import jax.numpy as jnp
from jax import lax
from jax.experimental import pallas as pl
from jax.experimental.pallas import tpu as pltpu
from jax.sharding import PartitionSpec as P

HEAD = 128
LOG2E = math.log2(math.e)
SCALE = 1.0 / math.sqrt(HEAD)
VMEM_LIMIT = 56 * 1024 * 1024
KEY_CHUNK = 512
ROW_CHUNK = 512

BF = jnp.bfloat16
F32 = jnp.float32


def dot_nt(a, b):
    return lax.dot_general(a, b, (((1,), (1,)), ((), ())), preferred_element_type=F32)


def dot_nn(a, b):
    return lax.dot_general(a, b, (((1,), (0,)), ((), ())), preferred_element_type=F32)


def dot_tn(a, b):
    return lax.dot_general(a, b, (((0,), (0,)), ((), ())), preferred_element_type=F32)


def split_sum(product):
    high = product.astype(BF)
    low = (product - high.astype(F32)).astype(BF)
    return high, low


def tile_grads(keys, values, queries, grads, lse_row, delta_row, mask):
    scores = dot_nt(keys, queries)
    probs = jnp.exp2(scores * (SCALE * LOG2E) - lse_row)
    if mask is not None:
        probs = jnp.where(mask, probs, 0.0)
    grad_probs = dot_nt(values, grads)
    grad_scores = (probs * (grad_probs - delta_row)).astype(BF)
    grad_value = dot_nn(probs.astype(BF), grads)
    grad_key = dot_nn(grad_scores, queries)
    grad_query = dot_tn(grad_scores, keys)
    return grad_query, grad_key, grad_value


def stacked_heads(ref, low, high, base, group, members):
    first = base + group * members * HEAD
    return jnp.concatenate(
        [ref[low:high, first + h * HEAD : first + (h + 1) * HEAD] for h in range(members)], axis=0
    )


def pack_rows(dest, heads, q_ref, do_ref, o_ref, lse_ref, out):
    rows, width = q_ref.shape
    all_heads = lse_ref.shape[1]
    lse_column = lax.broadcasted_iota(jnp.int32, (all_heads, HEAD), 0)
    lse_lane = lax.broadcasted_iota(jnp.int32, (all_heads, HEAD), 1)
    lane = lax.broadcasted_iota(jnp.int32, (rows, HEAD), 1)
    delta = jnp.zeros((rows, HEAD), F32)
    for h in range(heads):
        cols = slice(h * HEAD, (h + 1) * HEAD)
        product = do_ref[:, cols].astype(F32) * o_ref[:, cols].astype(F32)
        here = (lane == heads + h) | (lane == 2 * heads + h)
        delta = jnp.where(here, jnp.sum(product, axis=1, keepdims=True), delta)
    out[:, :width] = q_ref[...]
    out[:, width : 2 * width] = do_ref[...]
    lse_pick = jnp.where((lse_column == lse_lane + dest * heads) & (lse_lane < heads), 1.0, 0.0)
    lse = dot_nn(lse_ref[...], lse_pick.astype(BF))
    delta_high = delta.astype(BF).astype(F32)
    stats = jnp.where(lane < heads, lse, jnp.where(lane < 2 * heads, delta_high, delta - delta_high))
    out[:, 2 * width : 2 * width + HEAD] = stats.astype(BF)


def pack_kernel(me_ref, q_ref, do_ref, o_ref, lse_ref, k_ref, v_ref, pk_ref, pv_ref, kv_out, *outs):
    parts = len(outs)
    width = q_ref.shape[1] // parts
    narrow = k_ref.shape[1] // parts
    start = 2 * width + HEAD
    me = me_ref[0]
    kv_out[:, :narrow] = pk_ref[...]
    kv_out[:, narrow:] = pv_ref[...]
    for k, out in enumerate(outs):
        dest = me ^ k
        wide = pl.ds(pl.multiple_of(dest * width, HEAD), width)
        thin = pl.ds(pl.multiple_of(dest * narrow, HEAD), narrow)
        pack_rows(
            dest, width // HEAD, q_ref.at[:, wide], do_ref.at[:, wide], o_ref.at[:, wide], lse_ref, out
        )
        out[:, start : start + narrow] = k_ref[:, thin]
        out[:, start + narrow :] = v_ref[:, thin]


def prompt_kernel(members, me_ref, q_ref, do_ref, o_ref, lse_ref, *rest):
    kv_refs, (dq_ref, part_ref) = rest[:-2], rest[-2:]
    slots = len(kv_refs)
    rows = q_ref.shape[0]
    half = rows // 2
    narrow = kv_refs[0].shape[1] // 2
    groups = narrow // HEAD
    heads = lse_ref.shape[0]
    me = me_ref[0]
    count = members * half
    ones = jnp.ones((8, HEAD), BF)
    chunk_slots = max(1, min(slots, KEY_CHUNK // half))
    chunk = chunk_slots * half
    key_row = lax.broadcasted_iota(jnp.int32, (chunk, 1), 0)
    query_row = lax.broadcasted_iota(jnp.int32, (1, count), 1) % half
    stat_lane = lax.broadcasted_iota(jnp.int32, (half, HEAD), 1)
    spread = (
        lax.broadcasted_iota(jnp.int32, (heads, HEAD), 0) == lax.broadcasted_iota(jnp.int32, (heads, HEAD), 1)
    )
    all_lse = dot_tn(lse_ref[...], jnp.where(spread, 1.0, 0.0).astype(BF))
    for g in range(groups):
        queries, grads, lse_rows, delta_rows = [], [], [], []
        for s in range(2):
            low, high = s * half, (s + 1) * half
            queries.append(stacked_heads(q_ref, low, high, 0, g, members))
            grads.append(stacked_heads(do_ref, low, high, 0, g, members))
            outs = stacked_heads(o_ref, low, high, 0, g, members)
            up, down = split_sum(grads[s].astype(F32) * outs.astype(F32))
            delta_rows.append((dot_nt(ones, up) + dot_nt(ones, down))[0:1])
            lse = all_lse[low:high]
            picked = jnp.concatenate(
                [jnp.where(stat_lane == g * members + h, lse, 0.0) for h in range(members)], axis=0
            )
            lse_rows.append(dot_nt(ones, picked.astype(BF))[0:1] * LOG2E)
        grad_queries = [None, None]
        for side in range(2):
            for c in range(slots // chunk_slots):
                owned = kv_refs[c * chunk_slots : (c + 1) * chunk_slots]
                span = slice(side * half, (side + 1) * half)
                keys = jnp.concatenate([r[span, g * HEAD : (g + 1) * HEAD] for r in owned], axis=0)
                values = jnp.concatenate(
                    [r[span, narrow + g * HEAD : narrow + (g + 1) * HEAD] for r in owned], axis=0
                )
                owner = me ^ (c * chunk_slots + key_row // half)
                offset = key_row % half
                grad_key = grad_value = None
                for s in (1, 0) if side == 0 else (1,):
                    mask = None
                    if s == side:
                        ahead = owner - me if side == 0 else me - owner
                        mask = ahead * half + offset <= query_row
                    dq, dk, dv = tile_grads(
                        keys, values, queries[s], grads[s], lse_rows[s], delta_rows[s], mask
                    )
                    grad_queries[s] = dq if grad_queries[s] is None else grad_queries[s] + dq
                    grad_key = dk if grad_key is None else grad_key + dk
                    grad_value = dv if grad_value is None else grad_value + dv
                grad_key = grad_key * SCALE
                for t in range(chunk_slots):
                    piece = slice(t * half, (t + 1) * half)
                    slot = c * chunk_slots + t
                    for total, at in ((grad_key, g * HEAD), (grad_value, narrow + g * HEAD)):
                        cols = slice(at, at + HEAD)
                        part_ref[slot, span, cols] = total[piece]
        for s in range(2):
            result = (grad_queries[s] * SCALE).astype(BF)
            for h in range(members):
                first = (g * members + h) * HEAD
                dq_ref[s * half : (s + 1) * half, first : first + HEAD] = result[h * half : (h + 1) * half]


def roll_kernel(parts, slots, members, me_ref, *rest):
    packs, rest = rest[:parts], rest[parts:]
    kv_refs, rest = rest[:slots], rest[slots:]
    part_ref, even_ref, odd_ref = rest[:3]
    backs = rest[3:]
    me = me_ref[0]
    rows = packs[0].shape[0]
    kv_rows = kv_refs[0].shape[0]
    narrow = kv_refs[0].shape[1] // 2
    groups = narrow // HEAD
    heads = groups * members
    width = heads * HEAD
    block = members * rows
    count = parts * block
    stat_row = lax.broadcasted_iota(jnp.int32, (8, HEAD), 0)
    stat_lane = lax.broadcasted_iota(jnp.int32, (8, HEAD), 1)
    pick = jnp.where(
        ((stat_row == 0) & (stat_lane < heads))
        | ((stat_row == 1) & (stat_lane >= heads) & (stat_lane < 3 * heads)),
        1.0,
        0.0,
    ).astype(BF)
    lane_head = lax.broadcasted_iota(jnp.int32, (rows, HEAD), 1) % heads
    chunk_slots = max(1, min(slots, KEY_CHUNK // kv_rows))
    row_chunk = min(count, ROW_CHUNK)
    own_key = lax.broadcasted_iota(jnp.int32, (parts * rows, 1), 0)
    own_key_pos = (me ^ (own_key // rows)) * rows + own_key % rows
    own_query = lax.broadcasted_iota(jnp.int32, (1, count), 1)
    own_query_pos = (me ^ (own_query // block)) * rows + own_query % rows
    for g in range(groups):
        queries = jnp.concatenate([stacked_heads(p, 0, rows, 0, g, members) for p in packs], axis=0)
        grads = jnp.concatenate([stacked_heads(p, 0, rows, width, g, members) for p in packs], axis=0)
        picked = []
        for p in packs:
            stats = p[:, 2 * width : 2 * width + HEAD]
            for h in range(members):
                picked.append(jnp.where(lane_head == g * members + h, stats, jnp.zeros_like(stats)))
        stat_rows = dot_nt(pick, jnp.concatenate(picked, axis=0))
        lse_row = stat_rows[0:1] * LOG2E
        delta_row = stat_rows[1:2]
        first = 2 * width + HEAD + g * HEAD
        own_keys = jnp.concatenate([p[:, first : first + HEAD] for p in packs], axis=0)
        own_values = jnp.concatenate([p[:, first + narrow : first + narrow + HEAD] for p in packs], axis=0)
        grad_query, own_dk, own_dv = tile_grads(
            own_keys, own_values, queries, grads, lse_row, delta_row, own_key_pos <= own_query_pos
        )
        own_dk = (own_dk * SCALE).astype(BF)
        own_dv = own_dv.astype(BF)
        for k, back in enumerate(backs):
            piece = slice(k * rows, (k + 1) * rows)
            back[:, width + g * HEAD : width + (g + 1) * HEAD] = own_dk[piece]
            back[:, width + narrow + g * HEAD : width + narrow + (g + 1) * HEAD] = own_dv[piece]
        grad_rows = [grad_query[r : r + row_chunk] for r in range(0, count, row_chunk)]
        for c in range(slots // chunk_slots):
            owned = kv_refs[c * chunk_slots : (c + 1) * chunk_slots]
            keys = jnp.concatenate([r[:, g * HEAD : (g + 1) * HEAD] for r in owned], axis=0)
            values = jnp.concatenate(
                [r[:, narrow + g * HEAD : narrow + (g + 1) * HEAD] for r in owned], axis=0
            )
            grad_key = grad_value = None
            for i in range(count // row_chunk):
                piece = slice(i * row_chunk, (i + 1) * row_chunk)
                dq, dk, dv = tile_grads(
                    keys, values, queries[piece], grads[piece], lse_row[:, piece], delta_row[:, piece], None
                )
                grad_rows[i] = grad_rows[i] + dq
                grad_key = dk if grad_key is None else grad_key + dk
                grad_value = dv if grad_value is None else grad_value + dv
            grad_key = grad_key * SCALE
            for t in range(chunk_slots):
                slot = c * chunk_slots + t
                piece = slice(t * kv_rows, (t + 1) * kv_rows)
                for total, base in ((grad_key, 0), (grad_value, narrow)):
                    cols = slice(base + g * HEAD, base + (g + 1) * HEAD)
                    value = total[piece] + part_ref[slot, :, cols]
                    if slot % 2 == 0:
                        even_ref[slot // 2, :, cols] = value
                    else:
                        odd_ref[slot // 2, :, cols] = value.astype(BF)
        result = jnp.concatenate([(r * SCALE).astype(BF) for r in grad_rows], axis=0)
        for k, back in enumerate(backs):
            for h in range(members):
                start = k * block + h * rows
                first = (g * members + h) * HEAD
                back[:, first : first + HEAD] = result[start : start + rows]


def add_kernel(even_ref, got_ref, own_ref, *outs):
    own_ref[...] = even_ref[0] + got_ref[0].astype(F32)
    for t, out in enumerate(outs):
        out[...] = (even_ref[t + 1] + got_ref[t + 1].astype(F32)).astype(BF)


def final_kernel(parts, others, me_ref, own_ref, *rest):
    got, rest = rest[:others], rest[others:]
    backs, outs = rest[:parts], rest[parts:]
    pk_ref, pv_ref, rq_ref, rk_ref, rv_ref = outs
    me = me_ref[0]
    total = own_ref[...]
    for r in got:
        total = total + r[...].astype(F32)
    narrow = pk_ref.shape[1]
    pk_ref[...] = total[:, :narrow].astype(BF)
    pv_ref[...] = total[:, narrow:].astype(BF)
    width = rq_ref.shape[1] // parts
    for k, back in enumerate(backs):
        dest = me ^ k
        rq_ref[:, pl.ds(pl.multiple_of(dest * width, HEAD), width)] = back[:, :width]
        thin = pl.ds(pl.multiple_of(dest * narrow, HEAD), narrow)
        rk_ref[:, thin] = back[:, width : width + narrow]
        rv_ref[:, thin] = back[:, width + narrow :]


VMEM = pl.BlockSpec(memory_space=pltpu.VMEM)
SMEM = pl.BlockSpec(memory_space=pltpu.SMEM)


def call(kernel, name, outs, args, scalar=True):
    return pl.pallas_call(
        kernel,
        name=name,
        out_shape=outs,
        in_specs=[SMEM] * scalar + [VMEM] * (len(args) - scalar),
        out_specs=[VMEM] * len(outs),
        compiler_params=pltpu.CompilerParams(vmem_limit_bytes=VMEM_LIMIT),
        cost_estimate=pl.CostEstimate(flops=0, bytes_accessed=0, transcendentals=0),
    )(*args)


def shape(dims, dtype):
    return jax.ShapeDtypeStruct(dims, dtype)


def swap(x, axis, k):
    n = lax.axis_size(axis)
    return lax.ppermute(x, axis, [(i, i ^ k) for i in range(n)])


def on_device(
    prompt_query,
    prompt_key_rows,
    prompt_value_rows,
    prompt_dout,
    prompt_out,
    prompt_lse,
    roll_query,
    rollout_key_rows,
    rollout_value_rows,
    roll_dout,
    roll_out,
    roll_lse,
):
    slots = lax.axis_size("ctx")
    parts = lax.axis_size("roll")
    ctx_id = lax.axis_index("ctx").astype(jnp.int32).reshape(1)
    roll_id = lax.axis_index("roll").astype(jnp.int32).reshape(1)
    prompt_rows, width = prompt_query.shape
    narrow = prompt_key_rows.shape[1]
    members = width // narrow
    heads = width // HEAD
    rows = roll_query.shape[0]
    packed = 2 * width + HEAD + 2 * narrow

    kv, *packs = call(
        pack_kernel,
        "pack",
        [shape((prompt_rows, 2 * narrow), BF)] + [shape((rows, packed), BF)] * parts,
        (
            roll_id,
            roll_query,
            roll_dout,
            roll_out,
            roll_lse,
            rollout_key_rows,
            rollout_value_rows,
            prompt_key_rows,
            prompt_value_rows,
        ),
    )
    got = [swap(x, "roll", k) if k else x for k, x in enumerate(packs)]
    blocks = [None] * slots
    for s in range(0, slots, 2):
        blocks[s] = swap(kv, "ctx", s) if s else kv
        blocks[s + 1] = swap(blocks[s], "ctx", 1)

    prompt_dq, part = call(
        functools.partial(prompt_kernel, members),
        "prompt_grads",
        [shape((prompt_rows, width), BF), shape((slots, prompt_rows, 2 * narrow), F32)],
        (ctx_id, prompt_query, prompt_dout, prompt_out, prompt_lse.T, *blocks),
    )
    even, odd, *backs = call(
        functools.partial(roll_kernel, parts, slots, members),
        "roll_grads",
        [
            shape((slots // 2, prompt_rows, 2 * narrow), F32),
            shape((slots // 2, prompt_rows, 2 * narrow), BF),
        ]
        + [shape((rows, width + 2 * narrow), BF)] * parts,
        (roll_id, *got, *blocks, part),
    )
    odd_got = swap(odd, "ctx", 1)
    backs = [swap(x, "roll", k) if k else x for k, x in enumerate(backs)]
    own, *sums = call(
        add_kernel,
        "pair_sum",
        [shape((prompt_rows, 2 * narrow), F32)] + [shape((prompt_rows, 2 * narrow), BF)] * (slots // 2 - 1),
        (even, odd_got),
        scalar=False,
    )
    sums = [swap(x, "ctx", 2 * (t + 1)) for t, x in enumerate(sums)]
    prompt_dk, prompt_dv, roll_dq, roll_dk, roll_dv = call(
        functools.partial(final_kernel, parts, len(sums)),
        "finish",
        [
            shape((prompt_rows, narrow), BF),
            shape((prompt_rows, narrow), BF),
            shape((rows, parts * width), BF),
            shape((rows, parts * narrow), BF),
            shape((rows, parts * narrow), BF),
        ],
        (roll_id, own, *sums, *backs),
    )
    return prompt_dq, prompt_dk, prompt_dv, roll_dq, roll_dk, roll_dv


def solution(mesh):
    both = P(("ctx", "roll"), None)
    split = P("ctx", "roll")
    return jax.shard_map(
        on_device,
        mesh=mesh,
        in_specs=(split,) * 6 + (both,) * 6,
        out_specs=(split,) * 3 + (both,) * 3,
        check_vma=False,
    )
```

```python
import functools
import math

import jax
import jax.numpy as jnp
from jax import lax
from jax.experimental import pallas as pl
from jax.experimental.pallas import tpu as pltpu
from jax.sharding import PartitionSpec as P

HEAD = 128
LOG2E = math.log2(math.e)
SCALE = 1.0 / math.sqrt(HEAD)
VMEM_LIMIT = 28 * 1024 * 1024
KEY_CHUNK = 512

BF = jnp.bfloat16
F32 = jnp.float32


def dot_nt(a, b):
    return lax.dot_general(a, b, (((1,), (1,)), ((), ())), preferred_element_type=F32)


def dot_nn(a, b):
    return lax.dot_general(a, b, (((1,), (0,)), ((), ())), preferred_element_type=F32)


def dot_tn(a, b):
    return lax.dot_general(a, b, (((0,), (0,)), ((), ())), preferred_element_type=F32)


def split_sum(product):
    high = product.astype(BF)
    low = (product - high.astype(F32)).astype(BF)
    return high, low


def tile_grads(keys, values, queries, grads, lse_row, delta_row, mask):
    scores = dot_nt(keys, queries)
    probs = jnp.exp2(scores * (SCALE * LOG2E) - lse_row)
    if mask is not None:
        probs = jnp.where(mask, probs, 0.0)
    grad_probs = dot_nt(values, grads)
    grad_scores = (probs * (grad_probs - delta_row)).astype(BF)
    grad_value = dot_nn(probs.astype(BF), grads)
    grad_key = dot_nn(grad_scores, queries)
    grad_query = dot_nn(keys.T, grad_scores)
    return grad_query, grad_key, grad_value


def stacked_heads(ref, low, high, base, group, members):
    first = base + group * members * HEAD
    return jnp.concatenate(
        [ref[low:high, first + h * HEAD : first + (h + 1) * HEAD] for h in range(members)], axis=0
    )


def stat_rows(packs, group, members, heads, width):
    rows = packs[0].shape[0]
    stat_row = lax.broadcasted_iota(jnp.int32, (8, HEAD), 0)
    stat_lane = lax.broadcasted_iota(jnp.int32, (8, HEAD), 1)
    pick = jnp.where(
        ((stat_row == 0) & (stat_lane < heads))
        | ((stat_row == 1) & (stat_lane >= heads) & (stat_lane < 3 * heads)),
        1.0,
        0.0,
    ).astype(BF)
    lane_head = lax.broadcasted_iota(jnp.int32, (rows, HEAD), 1) % heads
    picked = []
    for p in packs:
        stats = p[:, 2 * width : 2 * width + HEAD]
        for h in range(members):
            picked.append(jnp.where(lane_head == group * members + h, stats, jnp.zeros_like(stats)))
    both = dot_nt(pick, jnp.concatenate(picked, axis=0))
    return both[0:1] * LOG2E, both[1:2]


def pack_rows(dest, heads, q_ref, do_ref, o_ref, lse_ref, out):
    rows, width = q_ref.shape
    all_heads = lse_ref.shape[1]
    lse_column = lax.broadcasted_iota(jnp.int32, (all_heads, HEAD), 0)
    lse_lane = lax.broadcasted_iota(jnp.int32, (all_heads, HEAD), 1)
    lane = lax.broadcasted_iota(jnp.int32, (rows, HEAD), 1)
    delta = jnp.zeros((rows, HEAD), F32)
    for h in range(heads):
        cols = slice(h * HEAD, (h + 1) * HEAD)
        product = do_ref[:, cols].astype(F32) * o_ref[:, cols].astype(F32)
        here = (lane == heads + h) | (lane == 2 * heads + h)
        delta = jnp.where(here, jnp.sum(product, axis=1, keepdims=True), delta)
    out[:, :width] = q_ref[...]
    out[:, width : 2 * width] = do_ref[...]
    lse_pick = jnp.where((lse_column == lse_lane + dest * heads) & (lse_lane < heads), 1.0, 0.0)
    lse = dot_nn(lse_ref[...], lse_pick.astype(BF))
    delta_high = delta.astype(BF).astype(F32)
    stats = jnp.where(lane < heads, lse, jnp.where(lane < 2 * heads, delta_high, delta - delta_high))
    out[:, 2 * width : 2 * width + HEAD] = stats.astype(BF)


def pack_kernel(me_ref, q_ref, do_ref, o_ref, lse_ref, k_ref, v_ref, pk_ref, pv_ref, kv_out, *outs):
    parts = len(outs)
    width = q_ref.shape[1] // parts
    narrow = k_ref.shape[1] // parts
    start = 2 * width + HEAD
    me = me_ref[0]
    kv_out[:, :narrow] = pk_ref[...]
    kv_out[:, narrow:] = pv_ref[...]
    for k, out in enumerate(outs):
        dest = me ^ k
        wide = pl.ds(pl.multiple_of(dest * width, HEAD), width)
        thin = pl.ds(pl.multiple_of(dest * narrow, HEAD), narrow)
        pack_rows(
            dest, width // HEAD, q_ref.at[:, wide], do_ref.at[:, wide], o_ref.at[:, wide], lse_ref, out
        )
        out[:, start : start + narrow] = k_ref[:, thin]
        out[:, start + narrow :] = v_ref[:, thin]


def prompt_kernel(members, me_ref, q_ref, do_ref, o_ref, lse_ref, roll_ref, *rest):
    kv_refs, (dq_ref, part_ref, roll_dq_ref) = rest[:-3], rest[-3:]
    slots = len(kv_refs)
    rows = q_ref.shape[0]
    half = rows // 2
    narrow = kv_refs[0].shape[1] // 2
    groups = narrow // HEAD
    heads = lse_ref.shape[0]
    width = q_ref.shape[1]
    me = me_ref[0]
    count = members * half
    ones = jnp.ones((8, HEAD), BF)
    chunk_slots = max(1, min(slots, KEY_CHUNK // half))
    chunk = chunk_slots * half
    key_row = lax.broadcasted_iota(jnp.int32, (chunk, 1), 0)
    query_row = lax.broadcasted_iota(jnp.int32, (1, count), 1) % half
    stat_lane = lax.broadcasted_iota(jnp.int32, (half, HEAD), 1)
    spread = (
        lax.broadcasted_iota(jnp.int32, (heads, HEAD), 0) == lax.broadcasted_iota(jnp.int32, (heads, HEAD), 1)
    )
    all_lse = dot_tn(lse_ref[...], jnp.where(spread, 1.0, 0.0).astype(BF))
    for g in range(groups):
        queries, grads, lse_rows, delta_rows = [], [], [], []
        for s in range(2):
            low, high = s * half, (s + 1) * half
            queries.append(stacked_heads(q_ref, low, high, 0, g, members))
            grads.append(stacked_heads(do_ref, low, high, 0, g, members))
            outs = stacked_heads(o_ref, low, high, 0, g, members)
            up, down = split_sum(grads[s].astype(F32) * outs.astype(F32))
            delta_rows.append((dot_nt(ones, up) + dot_nt(ones, down))[0:1])
            lse = all_lse[low:high]
            picked = jnp.concatenate(
                [jnp.where(stat_lane == g * members + h, lse, 0.0) for h in range(members)], axis=0
            )
            lse_rows.append(dot_nt(ones, picked.astype(BF))[0:1] * LOG2E)
        queries.append(stacked_heads(roll_ref, 0, roll_ref.shape[0], 0, g, members))
        grads.append(stacked_heads(roll_ref, 0, roll_ref.shape[0], width, g, members))
        lse_row, delta_row = stat_rows([roll_ref], g, members, heads, width)
        lse_rows.append(lse_row)
        delta_rows.append(delta_row)
        grad_queries = [None, None, None]
        for side in range(2):
            for c in range(slots // chunk_slots):
                owned = kv_refs[c * chunk_slots : (c + 1) * chunk_slots]
                span = slice(side * half, (side + 1) * half)
                keys = jnp.concatenate([r[span, g * HEAD : (g + 1) * HEAD] for r in owned], axis=0)
                values = jnp.concatenate(
                    [r[span, narrow + g * HEAD : narrow + (g + 1) * HEAD] for r in owned], axis=0
                )
                owner = me ^ (c * chunk_slots + key_row // half)
                offset = key_row % half
                grad_key = grad_value = None
                for s in (1, 0, 2) if side == 0 else (1, 2):
                    mask = None
                    if s == side:
                        ahead = owner - me if side == 0 else me - owner
                        mask = ahead * half + offset <= query_row
                    dq, dk, dv = tile_grads(
                        keys, values, queries[s], grads[s], lse_rows[s], delta_rows[s], mask
                    )
                    grad_queries[s] = dq if grad_queries[s] is None else grad_queries[s] + dq
                    grad_key = dk if grad_key is None else grad_key + dk
                    grad_value = dv if grad_value is None else grad_value + dv
                grad_key = grad_key * SCALE
                for t in range(chunk_slots):
                    piece = slice(t * half, (t + 1) * half)
                    slot = c * chunk_slots + t
                    for total, at in ((grad_key, g * HEAD), (grad_value, narrow + g * HEAD)):
                        cols = slice(at, at + HEAD)
                        part_ref[slot, span, cols] = total[piece]
        for s in range(2):
            result = (grad_queries[s] * SCALE).T.astype(BF)
            for h in range(members):
                first = (g * members + h) * HEAD
                dq_ref[s * half : (s + 1) * half, first : first + HEAD] = result[h * half : (h + 1) * half]
        roll_dq_ref[g] = grad_queries[2]


def roll_kernel(parts, slots, members, me_ref, *rest):
    packs, rest = rest[:parts], rest[parts:]
    kv_refs, rest = rest[:slots], rest[slots:]
    part_ref, roll_dq_ref, even_ref, odd_ref = rest[:4]
    backs = rest[4:]
    me = me_ref[0]
    rows = packs[0].shape[0]
    kv_rows = kv_refs[0].shape[0]
    narrow = kv_refs[0].shape[1] // 2
    groups = narrow // HEAD
    heads = groups * members
    width = heads * HEAD
    block = members * rows
    count = parts * block
    chunk_slots = max(1, min(slots, KEY_CHUNK // kv_rows))
    own_key = lax.broadcasted_iota(jnp.int32, (parts * rows, 1), 0)
    own_key_pos = (me ^ (own_key // rows)) * rows + own_key % rows
    own_query = lax.broadcasted_iota(jnp.int32, (1, count), 1)
    own_query_pos = (me ^ (own_query // block)) * rows + own_query % rows
    for g in range(groups):
        queries = jnp.concatenate([stacked_heads(p, 0, rows, 0, g, members) for p in packs], axis=0)
        grads = jnp.concatenate([stacked_heads(p, 0, rows, width, g, members) for p in packs], axis=0)
        lse_row, delta_row = stat_rows(packs, g, members, heads, width)
        first = 2 * width + HEAD + g * HEAD
        own_keys = jnp.concatenate([p[:, first : first + HEAD] for p in packs], axis=0)
        own_values = jnp.concatenate([p[:, first + narrow : first + narrow + HEAD] for p in packs], axis=0)
        grad_query, own_dk, own_dv = tile_grads(
            own_keys, own_values, queries, grads, lse_row, delta_row, own_key_pos <= own_query_pos
        )
        own_dk = (own_dk * SCALE).astype(BF)
        own_dv = own_dv.astype(BF)
        for k, back in enumerate(backs):
            piece = slice(k * rows, (k + 1) * rows)
            back[:, width + g * HEAD : width + (g + 1) * HEAD] = own_dk[piece]
            back[:, width + narrow + g * HEAD : width + narrow + (g + 1) * HEAD] = own_dv[piece]
        own_grad = grad_query[:, :block] + roll_dq_ref[g]
        others = slice(block, count)
        other_grad = grad_query[:, others]
        for c in range(slots // chunk_slots):
            owned = kv_refs[c * chunk_slots : (c + 1) * chunk_slots]
            keys = jnp.concatenate([r[:, g * HEAD : (g + 1) * HEAD] for r in owned], axis=0)
            values = jnp.concatenate(
                [r[:, narrow + g * HEAD : narrow + (g + 1) * HEAD] for r in owned], axis=0
            )
            dq, grad_key, grad_value = tile_grads(
                keys, values, queries[others], grads[others], lse_row[:, others], delta_row[:, others], None
            )
            other_grad = other_grad + dq
            grad_key = grad_key * SCALE
            for t in range(chunk_slots):
                slot = c * chunk_slots + t
                piece = slice(t * kv_rows, (t + 1) * kv_rows)
                for total, base in ((grad_key, 0), (grad_value, narrow)):
                    cols = slice(base + g * HEAD, base + (g + 1) * HEAD)
                    value = total[piece] + part_ref[slot, :, cols]
                    if slot % 2 == 0:
                        even_ref[slot // 2, :, cols] = value
                    else:
                        odd_ref[slot // 2, :, cols] = value.astype(BF)
        result = jnp.concatenate([(r * SCALE).T.astype(BF) for r in (own_grad, other_grad)], axis=0)
        for k, back in enumerate(backs):
            for h in range(members):
                start = k * block + h * rows
                first = (g * members + h) * HEAD
                back[:, first : first + HEAD] = result[start : start + rows]


def unpack_kernel(me_ref, *rest):
    backs, (rq_ref, rk_ref, rv_ref) = rest[:-3], rest[-3:]
    me = me_ref[0]
    width = rq_ref.shape[1] // len(backs)
    narrow = rk_ref.shape[1] // len(backs)
    for k, back in enumerate(backs):
        dest = me ^ k
        rq_ref[:, pl.ds(pl.multiple_of(dest * width, HEAD), width)] = back[:, :width]
        thin = pl.ds(pl.multiple_of(dest * narrow, HEAD), narrow)
        rk_ref[:, thin] = back[:, width : width + narrow]
        rv_ref[:, thin] = back[:, width + narrow :]


VMEM = pl.BlockSpec(memory_space=pltpu.VMEM)
SMEM = pl.BlockSpec(memory_space=pltpu.SMEM)


def call(kernel, name, outs, args, scalar=True, unread=0):
    return pl.pallas_call(
        kernel,
        name=name,
        out_shape=outs,
        in_specs=[SMEM] * scalar
        + [VMEM] * (len(args) - scalar - unread)
        + [pl.BlockSpec(memory_space=pl.ANY)] * unread,
        out_specs=[VMEM] * len(outs),
        compiler_params=pltpu.CompilerParams(vmem_limit_bytes=VMEM_LIMIT),
        cost_estimate=pl.CostEstimate(flops=0, bytes_accessed=0, transcendentals=0),
    )(*args)


def shape(dims, dtype):
    return jax.ShapeDtypeStruct(dims, dtype)


def vmem_shape(dims, dtype):
    return pltpu.VMEM(dims, dtype)


def swap(x, axis, k):
    n = lax.axis_size(axis)
    return lax.ppermute(x, axis, [(i, i ^ k) for i in range(n)])


def in_hbm(x):
    return pltpu.with_memory_space_constraint(x, pltpu.HBM)


def in_vmem(x):
    return pltpu.with_memory_space_constraint(x, pltpu.VMEM)


def on_device(
    prompt_query,
    prompt_key_rows,
    prompt_value_rows,
    prompt_dout,
    prompt_out,
    prompt_lse,
    roll_query,
    rollout_key_rows,
    rollout_value_rows,
    roll_dout,
    roll_out,
    roll_lse,
):
    slots = lax.axis_size("ctx")
    parts = lax.axis_size("roll")
    ctx_id = lax.axis_index("ctx").astype(jnp.int32).reshape(1)
    roll_id = lax.axis_index("roll").astype(jnp.int32).reshape(1)
    prompt_rows, width = prompt_query.shape
    narrow = prompt_key_rows.shape[1]
    members = width // narrow
    heads = width // HEAD
    rows = roll_query.shape[0]
    packed = 2 * width + HEAD + 2 * narrow

    kv, *packs = call(
        pack_kernel,
        "pack",
        [vmem_shape((prompt_rows, 2 * narrow), BF)] + [vmem_shape((rows, packed), BF)] * parts,
        (
            roll_id,
            *map(
                in_hbm,
                (
                    roll_query,
                    roll_dout,
                    roll_out,
                    roll_lse,
                    rollout_key_rows,
                    rollout_value_rows,
                    prompt_key_rows,
                    prompt_value_rows,
                ),
            ),
        ),
    )
    got = [swap(x, "roll", k) if k else x for k, x in enumerate(packs)]
    blocks = [None] * slots
    for s in range(0, slots, 2):
        blocks[s] = swap(kv, "ctx", s) if s else kv
        blocks[s + 1] = swap(blocks[s], "ctx", 1)
    blocks = [in_vmem(x) for x in blocks]

    prompt_dq, part, roll_own_dq = call(
        functools.partial(prompt_kernel, members),
        "prompt_grads",
        [
            shape((prompt_rows, width), BF),
            vmem_shape((slots, prompt_rows, 2 * narrow), F32),
            vmem_shape((narrow // HEAD, HEAD, members * rows), F32),
        ],
        (ctx_id, prompt_query, prompt_dout, prompt_out, prompt_lse.T, in_vmem(packs[0]), *blocks),
    )
    even, odd, *backs = call(
        functools.partial(roll_kernel, parts, slots, members),
        "roll_grads",
        [
            vmem_shape((slots // 2, prompt_rows, 2 * narrow), F32),
            vmem_shape((slots // 2, prompt_rows, 2 * narrow), BF),
        ]
        + [vmem_shape((rows, width + 2 * narrow), BF)] * parts,
        (roll_id, *[in_vmem(x) for x in got], *blocks, in_vmem(part), in_vmem(roll_own_dq)),
    )
    odd_got = swap(odd, "ctx", 1)
    backs = [in_vmem(swap(x, "roll", k) if k else x) for k, x in enumerate(backs)]
    pair = [even[t] + odd_got[t].astype(F32) for t in range(slots // 2)]
    total = pair[0]
    for t in range(1, slots // 2):
        total = total + swap(pair[t].astype(BF), "ctx", 2 * t).astype(F32)
    prompt_dk, prompt_dv = total[:, :narrow].astype(BF), total[:, narrow:].astype(BF)
    roll_dq, roll_dk, roll_dv = call(
        unpack_kernel,
        "unpack",
        [
            shape((rows, parts * width), BF),
            shape((rows, parts * narrow), BF),
            shape((rows, parts * narrow), BF),
        ],
        (roll_id, *backs),
    )
    return prompt_dq, prompt_dk, prompt_dv, roll_dq, roll_dk, roll_dv


def solution(mesh):
    both = P(("ctx", "roll"), None)
    split = P("ctx", "roll")
    return jax.shard_map(
        on_device,
        mesh=mesh,
        in_specs=(split,) * 6 + (both,) * 6,
        out_specs=(split,) * 3 + (both,) * 3,
        check_vma=False,
    )
```

```python
import functools
import math

import jax
import jax.numpy as jnp
from jax import lax
from jax.experimental import pallas as pl
from jax.experimental.pallas import tpu as pltpu
from jax.sharding import PartitionSpec as P

HEAD = 128
LOG2E = math.log2(math.e)
SCALE = 1.0 / math.sqrt(HEAD)
VMEM_LIMIT = 28 * 1024 * 1024
KEY_CHUNK = 512

BF = jnp.bfloat16
F32 = jnp.float32


def dot_nt(a, b):
    return lax.dot_general(a, b, (((1,), (1,)), ((), ())), preferred_element_type=F32)


def dot_nn(a, b):
    return lax.dot_general(a, b, (((1,), (0,)), ((), ())), preferred_element_type=F32)


def dot_tn(a, b):
    return lax.dot_general(a, b, (((0,), (0,)), ((), ())), preferred_element_type=F32)


def split_sum(product):
    high = product.astype(BF)
    low = (product - high.astype(F32)).astype(BF)
    return high, low


def tile_grads(keys, values, queries, grads, lse_row, delta_row, mask):
    scores = dot_nt(keys, queries)
    probs = jnp.exp2(scores * (SCALE * LOG2E) - lse_row)
    if mask is not None:
        probs = jnp.where(mask, probs, 0.0)
    grad_probs = dot_nt(values, grads)
    grad_scores = (probs * (grad_probs - delta_row)).astype(BF)
    grad_value = dot_nn(probs.astype(BF), grads)
    grad_key = dot_nn(grad_scores, queries)
    grad_query = dot_nn(keys.T, grad_scores)
    return grad_query, grad_key, grad_value


def stacked_heads(ref, low, high, base, group, members):
    first = base + group * members * HEAD
    return jnp.concatenate(
        [ref[low:high, first + h * HEAD : first + (h + 1) * HEAD] for h in range(members)], axis=0
    )


def send_order(parts):
    return sorted(range(parts), key=lambda k: (k % 2, k))


def by_partner(refs):
    order = send_order(len(refs))
    return [refs[order.index(k)] for k in range(len(refs))]


def stat_rows(packs, group, members, heads, width):
    rows = packs[0].shape[0]
    stat_row = lax.broadcasted_iota(jnp.int32, (8, HEAD), 0)
    stat_lane = lax.broadcasted_iota(jnp.int32, (8, HEAD), 1)
    pick = jnp.where(
        ((stat_row == 0) & (stat_lane < heads))
        | ((stat_row == 1) & (stat_lane >= heads) & (stat_lane < 3 * heads)),
        1.0,
        0.0,
    ).astype(BF)
    lane_head = lax.broadcasted_iota(jnp.int32, (rows, HEAD), 1) % heads
    picked = []
    for p in packs:
        stats = p[:, 2 * width : 2 * width + HEAD]
        for h in range(members):
            picked.append(jnp.where(lane_head == group * members + h, stats, jnp.zeros_like(stats)))
    both = dot_nt(pick, jnp.concatenate(picked, axis=0))
    return both[0:1] * LOG2E, both[1:2]


def pack_rows(dest, heads, q_ref, do_ref, o_ref, lse_ref, out):
    rows, width = q_ref.shape
    all_heads = lse_ref.shape[1]
    lse_column = lax.broadcasted_iota(jnp.int32, (all_heads, HEAD), 0)
    lse_lane = lax.broadcasted_iota(jnp.int32, (all_heads, HEAD), 1)
    lane = lax.broadcasted_iota(jnp.int32, (rows, HEAD), 1)
    delta = jnp.zeros((rows, HEAD), F32)
    for h in range(heads):
        cols = slice(h * HEAD, (h + 1) * HEAD)
        product = do_ref[:, cols].astype(F32) * o_ref[:, cols].astype(F32)
        here = (lane == heads + h) | (lane == 2 * heads + h)
        delta = jnp.where(here, jnp.sum(product, axis=1, keepdims=True), delta)
    out[:, :width] = q_ref[...]
    out[:, width : 2 * width] = do_ref[...]
    lse_pick = jnp.where((lse_column == lse_lane + dest * heads) & (lse_lane < heads), 1.0, 0.0)
    lse = dot_nn(lse_ref[...], lse_pick.astype(BF))
    delta_high = delta.astype(BF).astype(F32)
    stats = jnp.where(lane < heads, lse, jnp.where(lane < 2 * heads, delta_high, delta - delta_high))
    out[:, 2 * width : 2 * width + HEAD] = stats.astype(BF)


def pack_kernel(me_ref, q_ref, do_ref, o_ref, lse_ref, k_ref, v_ref, pk_ref, pv_ref, kv_out, *outs):
    parts = len(outs)
    width = q_ref.shape[1] // parts
    narrow = k_ref.shape[1] // parts
    start = 2 * width + HEAD
    me = me_ref[0]
    kv_out[:, :narrow] = pk_ref[...]
    kv_out[:, narrow:] = pv_ref[...]
    for k, out in enumerate(outs):
        dest = me ^ k
        wide = pl.ds(pl.multiple_of(dest * width, HEAD), width)
        thin = pl.ds(pl.multiple_of(dest * narrow, HEAD), narrow)
        pack_rows(
            dest, width // HEAD, q_ref.at[:, wide], do_ref.at[:, wide], o_ref.at[:, wide], lse_ref, out
        )
        out[:, start : start + narrow] = k_ref[:, thin]
        out[:, start + narrow :] = v_ref[:, thin]


def prompt_kernel(members, me_ref, q_ref, do_ref, o_ref, lse_ref, roll_ref, *rest):
    kv_refs, (dq_ref, part_ref, roll_dq_ref) = rest[:-3], rest[-3:]
    slots = len(kv_refs)
    rows = q_ref.shape[0]
    half = rows // 2
    narrow = kv_refs[0].shape[1] // 2
    groups = narrow // HEAD
    heads = lse_ref.shape[0]
    width = q_ref.shape[1]
    me = me_ref[0]
    count = members * half
    ones = jnp.ones((8, HEAD), BF)
    chunk_slots = max(1, min(slots, KEY_CHUNK // half))
    chunk = chunk_slots * half
    key_row = lax.broadcasted_iota(jnp.int32, (chunk, 1), 0)
    query_row = lax.broadcasted_iota(jnp.int32, (1, count), 1) % half
    stat_lane = lax.broadcasted_iota(jnp.int32, (half, HEAD), 1)
    spread = (
        lax.broadcasted_iota(jnp.int32, (heads, HEAD), 0) == lax.broadcasted_iota(jnp.int32, (heads, HEAD), 1)
    )
    all_lse = dot_tn(lse_ref[...], jnp.where(spread, 1.0, 0.0).astype(BF))
    for g in range(groups):
        queries, grads, lse_rows, delta_rows = [], [], [], []
        for s in range(2):
            low, high = s * half, (s + 1) * half
            queries.append(stacked_heads(q_ref, low, high, 0, g, members))
            grads.append(stacked_heads(do_ref, low, high, 0, g, members))
            outs = stacked_heads(o_ref, low, high, 0, g, members)
            up, down = split_sum(grads[s].astype(F32) * outs.astype(F32))
            delta_rows.append((dot_nt(ones, up) + dot_nt(ones, down))[0:1])
            lse = all_lse[low:high]
            picked = jnp.concatenate(
                [jnp.where(stat_lane == g * members + h, lse, 0.0) for h in range(members)], axis=0
            )
            lse_rows.append(dot_nt(ones, picked.astype(BF))[0:1] * LOG2E)
        queries.append(stacked_heads(roll_ref, 0, roll_ref.shape[0], 0, g, members))
        grads.append(stacked_heads(roll_ref, 0, roll_ref.shape[0], width, g, members))
        lse_row, delta_row = stat_rows([roll_ref], g, members, heads, width)
        lse_rows.append(lse_row)
        delta_rows.append(delta_row)
        grad_queries = [None, None, None]
        for side in range(2):
            for c in range(slots // chunk_slots):
                owned = kv_refs[c * chunk_slots : (c + 1) * chunk_slots]
                span = slice(side * half, (side + 1) * half)
                keys = jnp.concatenate([r[span, g * HEAD : (g + 1) * HEAD] for r in owned], axis=0)
                values = jnp.concatenate(
                    [r[span, narrow + g * HEAD : narrow + (g + 1) * HEAD] for r in owned], axis=0
                )
                owner = me ^ (c * chunk_slots + key_row // half)
                offset = key_row % half
                grad_key = grad_value = None
                for s in (1, 0, 2) if side == 0 else (1, 2):
                    mask = None
                    if s == side:
                        ahead = owner - me if side == 0 else me - owner
                        mask = ahead * half + offset <= query_row
                    dq, dk, dv = tile_grads(
                        keys, values, queries[s], grads[s], lse_rows[s], delta_rows[s], mask
                    )
                    grad_queries[s] = dq if grad_queries[s] is None else grad_queries[s] + dq
                    grad_key = dk if grad_key is None else grad_key + dk
                    grad_value = dv if grad_value is None else grad_value + dv
                grad_key = grad_key * SCALE
                for t in range(chunk_slots):
                    piece = slice(t * half, (t + 1) * half)
                    slot = c * chunk_slots + t
                    for total, at in ((grad_key, g * HEAD), (grad_value, narrow + g * HEAD)):
                        cols = slice(at, at + HEAD)
                        part_ref[slot, span, cols] = total[piece]
        for s in range(2):
            result = (grad_queries[s] * SCALE).T.astype(BF)
            for h in range(members):
                first = (g * members + h) * HEAD
                dq_ref[s * half : (s + 1) * half, first : first + HEAD] = result[h * half : (h + 1) * half]
        roll_dq_ref[g] = grad_queries[2]


def roll_kernel(parts, slots, members, me_ref, *rest):
    packs, rest = by_partner(rest[:parts]), rest[parts:]
    kv_refs, rest = rest[:slots], rest[slots:]
    part_ref, roll_dq_ref, even_ref, odd_ref = rest[:4]
    backs = rest[4:]
    me = me_ref[0]
    rows = packs[0].shape[0]
    kv_rows = kv_refs[0].shape[0]
    narrow = kv_refs[0].shape[1] // 2
    groups = narrow // HEAD
    heads = groups * members
    width = heads * HEAD
    block = members * rows
    count = parts * block
    chunk_slots = max(1, min(slots, KEY_CHUNK // kv_rows))
    own_key = lax.broadcasted_iota(jnp.int32, (parts * rows, 1), 0)
    own_key_pos = (me ^ (own_key // rows)) * rows + own_key % rows
    own_query = lax.broadcasted_iota(jnp.int32, (1, count), 1)
    own_query_pos = (me ^ (own_query // block)) * rows + own_query % rows
    for g in range(groups):
        queries = jnp.concatenate([stacked_heads(p, 0, rows, 0, g, members) for p in packs], axis=0)
        grads = jnp.concatenate([stacked_heads(p, 0, rows, width, g, members) for p in packs], axis=0)
        lse_row, delta_row = stat_rows(packs, g, members, heads, width)
        first = 2 * width + HEAD + g * HEAD
        own_keys = jnp.concatenate([p[:, first : first + HEAD] for p in packs], axis=0)
        own_values = jnp.concatenate([p[:, first + narrow : first + narrow + HEAD] for p in packs], axis=0)
        grad_query, own_dk, own_dv = tile_grads(
            own_keys, own_values, queries, grads, lse_row, delta_row, own_key_pos <= own_query_pos
        )
        own_dk = (own_dk * SCALE).astype(BF)
        own_dv = own_dv.astype(BF)
        for k, back in enumerate(backs):
            piece = slice(k * rows, (k + 1) * rows)
            back[:, width + g * HEAD : width + (g + 1) * HEAD] = own_dk[piece]
            back[:, width + narrow + g * HEAD : width + narrow + (g + 1) * HEAD] = own_dv[piece]
        own_grad = grad_query[:, :block] + roll_dq_ref[g]
        others = slice(block, count)
        other_grad = grad_query[:, others]
        for c in range(slots // chunk_slots):
            owned = kv_refs[c * chunk_slots : (c + 1) * chunk_slots]
            keys = jnp.concatenate([r[:, g * HEAD : (g + 1) * HEAD] for r in owned], axis=0)
            values = jnp.concatenate(
                [r[:, narrow + g * HEAD : narrow + (g + 1) * HEAD] for r in owned], axis=0
            )
            dq, grad_key, grad_value = tile_grads(
                keys, values, queries[others], grads[others], lse_row[:, others], delta_row[:, others], None
            )
            other_grad = other_grad + dq
            grad_key = grad_key * SCALE
            for t in range(chunk_slots):
                slot = c * chunk_slots + t
                piece = slice(t * kv_rows, (t + 1) * kv_rows)
                for total, base in ((grad_key, 0), (grad_value, narrow)):
                    cols = slice(base + g * HEAD, base + (g + 1) * HEAD)
                    value = total[piece] + part_ref[slot, :, cols]
                    if slot % 2 == 0:
                        even_ref[slot // 2, :, cols] = value
                    else:
                        odd_ref[slot // 2, :, cols] = value.astype(BF)
        result = jnp.concatenate([(r * SCALE).T.astype(BF) for r in (own_grad, other_grad)], axis=0)
        for k, back in enumerate(backs):
            for h in range(members):
                start = k * block + h * rows
                first = (g * members + h) * HEAD
                back[:, first : first + HEAD] = result[start : start + rows]


def unpack_kernel(me_ref, *rest):
    backs, (rq_ref, rk_ref, rv_ref) = by_partner(rest[:-3]), rest[-3:]
    me = me_ref[0]
    width = rq_ref.shape[1] // len(backs)
    narrow = rk_ref.shape[1] // len(backs)
    for k, back in enumerate(backs):
        dest = me ^ k
        rq_ref[:, pl.ds(pl.multiple_of(dest * width, HEAD), width)] = back[:, :width]
        thin = pl.ds(pl.multiple_of(dest * narrow, HEAD), narrow)
        rk_ref[:, thin] = back[:, width : width + narrow]
        rv_ref[:, thin] = back[:, width + narrow :]


VMEM = pl.BlockSpec(memory_space=pltpu.VMEM)
SMEM = pl.BlockSpec(memory_space=pltpu.SMEM)


def call(kernel, name, outs, args, scalar=True, unread=0):
    return pl.pallas_call(
        kernel,
        name=name,
        out_shape=outs,
        in_specs=[SMEM] * scalar
        + [VMEM] * (len(args) - scalar - unread)
        + [pl.BlockSpec(memory_space=pl.ANY)] * unread,
        out_specs=[VMEM] * len(outs),
        compiler_params=pltpu.CompilerParams(vmem_limit_bytes=VMEM_LIMIT),
        cost_estimate=pl.CostEstimate(flops=0, bytes_accessed=0, transcendentals=0),
    )(*args)


def shape(dims, dtype):
    return jax.ShapeDtypeStruct(dims, dtype)


def vmem_shape(dims, dtype):
    return pltpu.VMEM(dims, dtype)


def swap(x, axis, k):
    n = lax.axis_size(axis)
    return lax.ppermute(x, axis, [(i, i ^ k) for i in range(n)])


def in_hbm(x):
    return pltpu.with_memory_space_constraint(x, pltpu.HBM)


def in_vmem(x):
    return pltpu.with_memory_space_constraint(x, pltpu.VMEM)


def on_device(
    prompt_query,
    prompt_key_rows,
    prompt_value_rows,
    prompt_dout,
    prompt_out,
    prompt_lse,
    roll_query,
    rollout_key_rows,
    rollout_value_rows,
    roll_dout,
    roll_out,
    roll_lse,
):
    slots = lax.axis_size("ctx")
    parts = lax.axis_size("roll")
    ctx_id = lax.axis_index("ctx").astype(jnp.int32).reshape(1)
    roll_id = lax.axis_index("roll").astype(jnp.int32).reshape(1)
    prompt_rows, width = prompt_query.shape
    narrow = prompt_key_rows.shape[1]
    members = width // narrow
    heads = width // HEAD
    rows = roll_query.shape[0]
    packed = 2 * width + HEAD + 2 * narrow

    kv, *packs = call(
        pack_kernel,
        "pack",
        [vmem_shape((prompt_rows, 2 * narrow), BF)] + [vmem_shape((rows, packed), BF)] * parts,
        (
            roll_id,
            *map(
                in_hbm,
                (
                    roll_query,
                    roll_dout,
                    roll_out,
                    roll_lse,
                    rollout_key_rows,
                    rollout_value_rows,
                    prompt_key_rows,
                    prompt_value_rows,
                ),
            ),
        ),
    )
    got = [swap(x, "roll", k) if k else x for k, x in enumerate(packs)]
    blocks = [in_vmem(swap(kv, "ctx", s) if s else kv) for s in range(slots)]

    prompt_dq, part, roll_own_dq = call(
        functools.partial(prompt_kernel, members),
        "prompt_grads",
        [
            shape((prompt_rows, width), BF),
            vmem_shape((slots, prompt_rows, 2 * narrow), F32),
            vmem_shape((narrow // HEAD, HEAD, members * rows), F32),
        ],
        (ctx_id, *map(in_hbm, (prompt_query, prompt_dout, prompt_out, prompt_lse.T)), in_vmem(packs[0]), *blocks),
    )
    even, odd, *backs = call(
        functools.partial(roll_kernel, parts, slots, members),
        "roll_grads",
        [
            vmem_shape((slots // 2, prompt_rows, 2 * narrow), F32),
            vmem_shape((slots // 2, prompt_rows, 2 * narrow), BF),
        ]
        + [vmem_shape((rows, width + 2 * narrow), BF)] * parts,
        (roll_id, *[in_vmem(got[k]) for k in send_order(parts)], *blocks, in_vmem(part), in_vmem(roll_own_dq)),
    )
    odd_got = swap(odd, "ctx", 1)
    backs = [in_vmem(swap(x, "roll", k) if k else x) for k, x in enumerate(backs)]
    pair = [even[t] + odd_got[t].astype(F32) for t in range(slots // 2)]
    total = pair[0]
    for t in range(1, slots // 2):
        total = total + swap(pair[t].astype(BF), "ctx", 2 * t).astype(F32)
    prompt_dk, prompt_dv = total[:, :narrow].astype(BF), total[:, narrow:].astype(BF)
    roll_dq, roll_dk, roll_dv = call(
        unpack_kernel,
        "unpack",
        [
            shape((rows, parts * width), BF),
            shape((rows, parts * narrow), BF),
            shape((rows, parts * narrow), BF),
        ],
        (roll_id, *[backs[k] for k in send_order(parts)]),
    )
    return prompt_dq, prompt_dk, prompt_dv, roll_dq, roll_dk, roll_dv


def solution(mesh):
    both = P(("ctx", "roll"), None)
    split = P("ctx", "roll")
    return jax.shard_map(
        on_device,
        mesh=mesh,
        in_specs=(split,) * 6 + (both,) * 6,
        out_specs=(split,) * 3 + (both,) * 3,
        check_vma=False,
    )
```

```python
import functools
import math

import jax
import jax.numpy as jnp
from jax import lax
from jax.experimental import pallas as pl
from jax.experimental.pallas import tpu as pltpu
from jax.sharding import PartitionSpec as P

HEAD = 128
LOG2E = math.log2(math.e)
SCALE = 1.0 / math.sqrt(HEAD)
VMEM_LIMIT = 28 * 1024 * 1024
KEY_CHUNK = 256

BF = jnp.bfloat16
F32 = jnp.float32


def dot_nt(a, b):
    return lax.dot_general(a, b, (((1,), (1,)), ((), ())), preferred_element_type=F32)


def dot_nn(a, b):
    return lax.dot_general(a, b, (((1,), (0,)), ((), ())), preferred_element_type=F32)


def dot_tn(a, b):
    return lax.dot_general(a, b, (((0,), (0,)), ((), ())), preferred_element_type=F32)


def split_sum(product):
    high = product.astype(BF)
    low = (product - high.astype(F32)).astype(BF)
    return high, low


def tile_grads(keys, values, queries, grads, lse_row, delta_row, mask):
    scores = dot_nt(keys, queries)
    probs = jnp.exp2(scores * (SCALE * LOG2E) - lse_row)
    if mask is not None:
        probs = jnp.where(mask, probs, 0.0)
    grad_probs = dot_nt(values, grads)
    grad_scores = (probs * (grad_probs - delta_row)).astype(BF)
    grad_value = dot_nn(probs.astype(BF), grads)
    grad_key = dot_nn(grad_scores, queries)
    grad_query = dot_nn(keys.T, grad_scores)
    return grad_query, grad_key, grad_value


def stacked_heads(ref, low, high, base, group, members):
    first = base + group * members * HEAD
    return jnp.concatenate(
        [ref[low:high, first + h * HEAD : first + (h + 1) * HEAD] for h in range(members)], axis=0
    )


def send_order(parts):
    return sorted(range(parts), key=lambda k: (k % 2, k))


def by_partner(refs):
    order = send_order(len(refs))
    return [refs[order.index(k)] for k in range(len(refs))]


def stat_rows(packs, group, members, heads, width):
    rows = packs[0].shape[0]
    stat_row = lax.broadcasted_iota(jnp.int32, (8, HEAD), 0)
    stat_lane = lax.broadcasted_iota(jnp.int32, (8, HEAD), 1)
    pick = jnp.where(
        ((stat_row == 0) & (stat_lane < heads))
        | ((stat_row == 1) & (stat_lane >= heads) & (stat_lane < 3 * heads)),
        1.0,
        0.0,
    ).astype(BF)
    lane_head = lax.broadcasted_iota(jnp.int32, (rows, HEAD), 1) % heads
    picked = []
    for p in packs:
        stats = p[:, 2 * width : 2 * width + HEAD]
        for h in range(members):
            picked.append(jnp.where(lane_head == group * members + h, stats, jnp.zeros_like(stats)))
    both = dot_nt(pick, jnp.concatenate(picked, axis=0))
    return both[0:1] * LOG2E, both[1:2]


def pack_rows(dest, heads, q_ref, do_ref, o_ref, lse_ref, out):
    rows, width = q_ref.shape
    all_heads = lse_ref.shape[1]
    lse_column = lax.broadcasted_iota(jnp.int32, (all_heads, HEAD), 0)
    lse_lane = lax.broadcasted_iota(jnp.int32, (all_heads, HEAD), 1)
    lane = lax.broadcasted_iota(jnp.int32, (rows, HEAD), 1)
    delta = jnp.zeros((rows, HEAD), F32)
    for h in range(heads):
        cols = slice(h * HEAD, (h + 1) * HEAD)
        product = do_ref[:, cols].astype(F32) * o_ref[:, cols].astype(F32)
        here = (lane == heads + h) | (lane == 2 * heads + h)
        delta = jnp.where(here, jnp.sum(product, axis=1, keepdims=True), delta)
    out[:, :width] = q_ref[...]
    out[:, width : 2 * width] = do_ref[...]
    lse_pick = jnp.where((lse_column == lse_lane + dest * heads) & (lse_lane < heads), 1.0, 0.0)
    lse = dot_nn(lse_ref[...], lse_pick.astype(BF))
    delta_high = delta.astype(BF).astype(F32)
    stats = jnp.where(lane < heads, lse, jnp.where(lane < 2 * heads, delta_high, delta - delta_high))
    out[:, 2 * width : 2 * width + HEAD] = stats.astype(BF)


def pack_kernel(me_ref, q_ref, do_ref, o_ref, lse_ref, k_ref, v_ref, pk_ref, pv_ref, kv_out, *outs):
    parts = len(outs)
    width = q_ref.shape[1] // parts
    narrow = k_ref.shape[1] // parts
    start = 2 * width + HEAD
    me = me_ref[0]
    kv_out[:, :narrow] = pk_ref[...]
    kv_out[:, narrow:] = pv_ref[...]
    for k, out in enumerate(outs):
        dest = me ^ k
        wide = pl.ds(pl.multiple_of(dest * width, HEAD), width)
        thin = pl.ds(pl.multiple_of(dest * narrow, HEAD), narrow)
        pack_rows(
            dest, width // HEAD, q_ref.at[:, wide], do_ref.at[:, wide], o_ref.at[:, wide], lse_ref, out
        )
        out[:, start : start + narrow] = k_ref[:, thin]
        out[:, start + narrow :] = v_ref[:, thin]


def prompt_kernel(members, me_ref, q_ref, do_ref, o_ref, lse_ref, roll_ref, *rest):
    kv_refs, (dq_ref, part_ref, roll_dq_ref) = rest[:-3], rest[-3:]
    slots = len(kv_refs)
    rows = q_ref.shape[0]
    half = rows // 2
    narrow = kv_refs[0].shape[1] // 2
    groups = narrow // HEAD
    heads = lse_ref.shape[0]
    width = q_ref.shape[1]
    me = me_ref[0]
    count = members * half
    ones = jnp.ones((8, HEAD), BF)
    chunk_slots = max(1, min(slots, KEY_CHUNK // half))
    chunk = chunk_slots * half
    key_row = lax.broadcasted_iota(jnp.int32, (chunk, 1), 0)
    query_row = lax.broadcasted_iota(jnp.int32, (1, count), 1) % half
    stat_lane = lax.broadcasted_iota(jnp.int32, (half, HEAD), 1)
    spread = (
        lax.broadcasted_iota(jnp.int32, (heads, HEAD), 0) == lax.broadcasted_iota(jnp.int32, (heads, HEAD), 1)
    )
    all_lse = dot_tn(lse_ref[...], jnp.where(spread, 1.0, 0.0).astype(BF))
    for g in range(groups):
        queries, grads, lse_rows, delta_rows = [], [], [], []
        for s in range(2):
            low, high = s * half, (s + 1) * half
            queries.append(stacked_heads(q_ref, low, high, 0, g, members))
            grads.append(stacked_heads(do_ref, low, high, 0, g, members))
            outs = stacked_heads(o_ref, low, high, 0, g, members)
            up, down = split_sum(grads[s].astype(F32) * outs.astype(F32))
            delta_rows.append((dot_nt(ones, up) + dot_nt(ones, down))[0:1])
            lse = all_lse[low:high]
            picked = jnp.concatenate(
                [jnp.where(stat_lane == g * members + h, lse, 0.0) for h in range(members)], axis=0
            )
            lse_rows.append(dot_nt(ones, picked.astype(BF))[0:1] * LOG2E)
        queries.append(stacked_heads(roll_ref, 0, roll_ref.shape[0], 0, g, members))
        grads.append(stacked_heads(roll_ref, 0, roll_ref.shape[0], width, g, members))
        lse_row, delta_row = stat_rows([roll_ref], g, members, heads, width)
        lse_rows.append(lse_row)
        delta_rows.append(delta_row)
        grad_queries = [None, None, None]
        for side in range(2):
            for c in range(slots // chunk_slots):
                owned = kv_refs[c * chunk_slots : (c + 1) * chunk_slots]
                span = slice(side * half, (side + 1) * half)
                keys = jnp.concatenate([r[span, g * HEAD : (g + 1) * HEAD] for r in owned], axis=0)
                values = jnp.concatenate(
                    [r[span, narrow + g * HEAD : narrow + (g + 1) * HEAD] for r in owned], axis=0
                )
                owner = me ^ (c * chunk_slots + key_row // half)
                offset = key_row % half
                grad_key = grad_value = None
                for s in (1, 0, 2) if side == 0 else (1, 2):
                    mask = None
                    if s == side:
                        ahead = owner - me if side == 0 else me - owner
                        mask = ahead * half + offset <= query_row
                    dq, dk, dv = tile_grads(
                        keys, values, queries[s], grads[s], lse_rows[s], delta_rows[s], mask
                    )
                    grad_queries[s] = dq if grad_queries[s] is None else grad_queries[s] + dq
                    grad_key = dk if grad_key is None else grad_key + dk
                    grad_value = dv if grad_value is None else grad_value + dv
                grad_key = grad_key * SCALE
                for t in range(chunk_slots):
                    piece = slice(t * half, (t + 1) * half)
                    slot = c * chunk_slots + t
                    for total, at in ((grad_key, g * HEAD), (grad_value, narrow + g * HEAD)):
                        cols = slice(at, at + HEAD)
                        part_ref[slot, span, cols] = total[piece]
        for s in range(2):
            result = (grad_queries[s] * SCALE).T.astype(BF)
            for h in range(members):
                first = (g * members + h) * HEAD
                dq_ref[s * half : (s + 1) * half, first : first + HEAD] = result[h * half : (h + 1) * half]
        roll_dq_ref[g] = grad_queries[2]


def roll_kernel(parts, slots, members, me_ref, *rest):
    packs, rest = by_partner(rest[:parts]), rest[parts:]
    kv_refs, rest = rest[:slots], rest[slots:]
    part_ref, roll_dq_ref, even_ref, odd_ref = rest[:4]
    backs = rest[4:]
    me = me_ref[0]
    rows = packs[0].shape[0]
    kv_rows = kv_refs[0].shape[0]
    narrow = kv_refs[0].shape[1] // 2
    groups = narrow // HEAD
    heads = groups * members
    width = heads * HEAD
    block = members * rows
    count = parts * block
    chunk_slots = max(1, min(slots, KEY_CHUNK // kv_rows))
    own_key = lax.broadcasted_iota(jnp.int32, (parts * rows, 1), 0)
    own_key_pos = (me ^ (own_key // rows)) * rows + own_key % rows
    own_query = lax.broadcasted_iota(jnp.int32, (1, count), 1)
    own_query_pos = (me ^ (own_query // block)) * rows + own_query % rows
    for g in range(groups):
        queries = jnp.concatenate([stacked_heads(p, 0, rows, 0, g, members) for p in packs], axis=0)
        grads = jnp.concatenate([stacked_heads(p, 0, rows, width, g, members) for p in packs], axis=0)
        lse_row, delta_row = stat_rows(packs, g, members, heads, width)
        first = 2 * width + HEAD + g * HEAD
        own_keys = jnp.concatenate([p[:, first : first + HEAD] for p in packs], axis=0)
        own_values = jnp.concatenate([p[:, first + narrow : first + narrow + HEAD] for p in packs], axis=0)
        grad_query, own_dk, own_dv = tile_grads(
            own_keys, own_values, queries, grads, lse_row, delta_row, own_key_pos <= own_query_pos
        )
        own_dk = (own_dk * SCALE).astype(BF)
        own_dv = own_dv.astype(BF)
        for k, back in enumerate(backs):
            piece = slice(k * rows, (k + 1) * rows)
            back[:, width + g * HEAD : width + (g + 1) * HEAD] = own_dk[piece]
            back[:, width + narrow + g * HEAD : width + narrow + (g + 1) * HEAD] = own_dv[piece]
        own_grad = grad_query[:, :block] + roll_dq_ref[g]
        others = slice(block, count)
        other_grad = grad_query[:, others]
        for c in range(slots // chunk_slots):
            owned = kv_refs[c * chunk_slots : (c + 1) * chunk_slots]
            keys = jnp.concatenate([r[:, g * HEAD : (g + 1) * HEAD] for r in owned], axis=0)
            values = jnp.concatenate(
                [r[:, narrow + g * HEAD : narrow + (g + 1) * HEAD] for r in owned], axis=0
            )
            dq, grad_key, grad_value = tile_grads(
                keys, values, queries[others], grads[others], lse_row[:, others], delta_row[:, others], None
            )
            other_grad = other_grad + dq
            grad_key = grad_key * SCALE
            for t in range(chunk_slots):
                slot = c * chunk_slots + t
                piece = slice(t * kv_rows, (t + 1) * kv_rows)
                for total, base in ((grad_key, 0), (grad_value, narrow)):
                    cols = slice(base + g * HEAD, base + (g + 1) * HEAD)
                    value = total[piece] + part_ref[slot, :, cols]
                    if slot % 2 == 0:
                        even_ref[slot // 2, :, cols] = value
                    else:
                        odd_ref[slot // 2, :, cols] = value.astype(BF)
        result = jnp.concatenate([(r * SCALE).T.astype(BF) for r in (own_grad, other_grad)], axis=0)
        for k, back in enumerate(backs):
            for h in range(members):
                start = k * block + h * rows
                first = (g * members + h) * HEAD
                back[:, first : first + HEAD] = result[start : start + rows]


def unpack_kernel(sums, me_ref, *rest):
    (own_ref, *got), rest = rest[:sums], rest[sums:]
    backs, (pk_ref, pv_ref, rq_ref, rk_ref, rv_ref) = by_partner(rest[:-5]), rest[-5:]
    total = own_ref[...]
    for ref in got:
        total = total + ref[...].astype(F32)
    pk_ref[...] = total[:, : pk_ref.shape[1]].astype(BF)
    pv_ref[...] = total[:, pk_ref.shape[1] :].astype(BF)
    me = me_ref[0]
    width = rq_ref.shape[1] // len(backs)
    narrow = rk_ref.shape[1] // len(backs)
    for k, back in enumerate(backs):
        dest = me ^ k
        rq_ref[:, pl.ds(pl.multiple_of(dest * width, HEAD), width)] = back[:, :width]
        thin = pl.ds(pl.multiple_of(dest * narrow, HEAD), narrow)
        rk_ref[:, thin] = back[:, width : width + narrow]
        rv_ref[:, thin] = back[:, width + narrow :]


VMEM = pl.BlockSpec(memory_space=pltpu.VMEM)
SMEM = pl.BlockSpec(memory_space=pltpu.SMEM)


def call(kernel, name, outs, args, scalar=True, unread=0):
    return pl.pallas_call(
        kernel,
        name=name,
        out_shape=outs,
        in_specs=[SMEM] * scalar
        + [VMEM] * (len(args) - scalar - unread)
        + [pl.BlockSpec(memory_space=pl.ANY)] * unread,
        out_specs=[VMEM] * len(outs),
        compiler_params=pltpu.CompilerParams(vmem_limit_bytes=VMEM_LIMIT),
        cost_estimate=pl.CostEstimate(flops=0, bytes_accessed=0, transcendentals=0),
    )(*args)


def shape(dims, dtype):
    return jax.ShapeDtypeStruct(dims, dtype)


def vmem_shape(dims, dtype):
    return pltpu.VMEM(dims, dtype)


def swap(x, axis, k):
    n = lax.axis_size(axis)
    return lax.ppermute(x, axis, [(i, i ^ k) for i in range(n)])


def in_hbm(x):
    return pltpu.with_memory_space_constraint(x, pltpu.HBM)


def in_vmem(x):
    return pltpu.with_memory_space_constraint(x, pltpu.VMEM)


def on_device(
    prompt_query,
    prompt_key_rows,
    prompt_value_rows,
    prompt_dout,
    prompt_out,
    prompt_lse,
    roll_query,
    rollout_key_rows,
    rollout_value_rows,
    roll_dout,
    roll_out,
    roll_lse,
):
    slots = lax.axis_size("ctx")
    parts = lax.axis_size("roll")
    ctx_id = lax.axis_index("ctx").astype(jnp.int32).reshape(1)
    roll_id = lax.axis_index("roll").astype(jnp.int32).reshape(1)
    prompt_rows, width = prompt_query.shape
    narrow = prompt_key_rows.shape[1]
    members = width // narrow
    heads = width // HEAD
    rows = roll_query.shape[0]
    packed = 2 * width + HEAD + 2 * narrow

    kv, *packs = call(
        pack_kernel,
        "pack",
        [vmem_shape((prompt_rows, 2 * narrow), BF)] + [vmem_shape((rows, packed), BF)] * parts,
        (
            roll_id,
            *map(
                in_hbm,
                (
                    roll_query,
                    roll_dout,
                    roll_out,
                    roll_lse,
                    rollout_key_rows,
                    rollout_value_rows,
                    prompt_key_rows,
                    prompt_value_rows,
                ),
            ),
        ),
    )
    got = [swap(x, "roll", k) if k else x for k, x in enumerate(packs)]
    blocks = [kv]
    for s in range(1, slots):
        double = s % 2 and bin(s).count("1") > 2
        blocks.append(swap(blocks[s - 1], "ctx", 1) if double else swap(kv, "ctx", s))
    blocks = [in_vmem(x) for x in blocks]

    prompt_dq, part, roll_own_dq = call(
        functools.partial(prompt_kernel, members),
        "prompt_grads",
        [
            shape((prompt_rows, width), BF),
            vmem_shape((slots, prompt_rows, 2 * narrow), F32),
            vmem_shape((narrow // HEAD, HEAD, members * rows), F32),
        ],
        (ctx_id, *map(in_hbm, (prompt_query, prompt_dout, prompt_out, prompt_lse.T)), in_vmem(packs[0]), *blocks),
    )
    even, odd, *backs = call(
        functools.partial(roll_kernel, parts, slots, members),
        "roll_grads",
        [
            vmem_shape((slots // 2, prompt_rows, 2 * narrow), F32),
            vmem_shape((slots // 2, prompt_rows, 2 * narrow), BF),
        ]
        + [vmem_shape((rows, width + 2 * narrow), BF)] * parts,
        (roll_id, *[in_vmem(got[k]) for k in send_order(parts)], *blocks, in_vmem(part), in_vmem(roll_own_dq)),
    )
    odd_got = swap(odd, "ctx", 1)
    backs = [in_vmem(swap(x, "roll", k) if k else x) for k, x in enumerate(backs)]
    pair = [even[t] + odd_got[t].astype(F32) for t in range(slots // 2)]
    sums = [pair[0]] + [swap(pair[t].astype(BF), "ctx", 2 * t) for t in range(slots // 2 - 1, 0, -1)]
    prompt_dk, prompt_dv, roll_dq, roll_dk, roll_dv = call(
        functools.partial(unpack_kernel, len(sums)),
        "unpack",
        [
            shape((prompt_rows, narrow), BF),
            shape((prompt_rows, narrow), BF),
            shape((rows, parts * width), BF),
            shape((rows, parts * narrow), BF),
            shape((rows, parts * narrow), BF),
        ],
        (roll_id, *map(in_vmem, sums), *[backs[k] for k in send_order(parts)]),
    )
    return prompt_dq, prompt_dk, prompt_dv, roll_dq, roll_dk, roll_dv


def solution(mesh):
    both = P(("ctx", "roll"), None)
    split = P("ctx", "roll")
    return jax.shard_map(
        on_device,
        mesh=mesh,
        in_specs=(split,) * 6 + (both,) * 6,
        out_specs=(split,) * 3 + (both,) * 3,
        check_vma=False,
    )
```

```python
import functools
import math

import jax
import jax.numpy as jnp
from jax import lax
from jax.experimental import pallas as pl
from jax.experimental.pallas import tpu as pltpu
from jax.sharding import PartitionSpec as P

HEAD = 128
LOG2E = math.log2(math.e)
SCALE = 1.0 / math.sqrt(HEAD)
VMEM_LIMIT = 28 * 1024 * 1024
KEY_CHUNK = 256

BF = jnp.bfloat16
F32 = jnp.float32


def dot_nt(a, b):
    return lax.dot_general(a, b, (((1,), (1,)), ((), ())), preferred_element_type=F32)


def dot_nn(a, b):
    return lax.dot_general(a, b, (((1,), (0,)), ((), ())), preferred_element_type=F32)


def dot_tn(a, b):
    return lax.dot_general(a, b, (((0,), (0,)), ((), ())), preferred_element_type=F32)


def split_sum(product):
    high = product.astype(BF)
    low = (product - high.astype(F32)).astype(BF)
    return high, low


def tile_grads(keys, values, queries, grads, lse_row, delta_row, mask):
    scores = dot_nt(keys, queries)
    probs = jnp.exp2(scores * (SCALE * LOG2E) - lse_row)
    if mask is not None:
        probs = jnp.where(mask, probs, 0.0)
    grad_probs = dot_nt(values, grads)
    grad_scores = (probs * (grad_probs - delta_row)).astype(BF)
    grad_value = dot_nn(probs.astype(BF), grads)
    grad_key = dot_nn(grad_scores, queries)
    grad_query = dot_nn(keys.T, grad_scores)
    return grad_query, grad_key, grad_value


def stacked_heads(ref, low, high, base, group, members):
    first = base + group * members * HEAD
    return jnp.concatenate(
        [ref[low:high, first + h * HEAD : first + (h + 1) * HEAD] for h in range(members)], axis=0
    )


def send_order(parts):
    return sorted(range(parts), key=lambda k: (k % 2, k))


def return_order(parts):
    return sorted(range(parts), key=lambda k: (k > 0, k % 2 == 0, -k))


def by_partner(refs, order):
    return [refs[order.index(k)] for k in range(len(refs))]


def stat_rows(packs, group, members, heads, width):
    rows = packs[0].shape[0]
    stat_row = lax.broadcasted_iota(jnp.int32, (8, HEAD), 0)
    stat_lane = lax.broadcasted_iota(jnp.int32, (8, HEAD), 1)
    pick = jnp.where(
        ((stat_row == 0) & (stat_lane < heads))
        | ((stat_row == 1) & (stat_lane >= heads) & (stat_lane < 3 * heads)),
        1.0,
        0.0,
    ).astype(BF)
    lane_head = lax.broadcasted_iota(jnp.int32, (rows, HEAD), 1) % heads
    picked = []
    for p in packs:
        stats = p[:, 2 * width : 2 * width + HEAD]
        for h in range(members):
            picked.append(jnp.where(lane_head == group * members + h, stats, jnp.zeros_like(stats)))
    both = dot_nt(pick, jnp.concatenate(picked, axis=0))
    return both[0:1] * LOG2E, both[1:2]


def pack_rows(dest, heads, q_ref, do_ref, o_ref, lse_ref, out):
    rows, width = q_ref.shape
    all_heads = lse_ref.shape[1]
    lse_column = lax.broadcasted_iota(jnp.int32, (all_heads, HEAD), 0)
    lse_lane = lax.broadcasted_iota(jnp.int32, (all_heads, HEAD), 1)
    lane = lax.broadcasted_iota(jnp.int32, (rows, HEAD), 1)
    delta = jnp.zeros((rows, HEAD), F32)
    for h in range(heads):
        cols = slice(h * HEAD, (h + 1) * HEAD)
        product = do_ref[:, cols].astype(F32) * o_ref[:, cols].astype(F32)
        here = (lane == heads + h) | (lane == 2 * heads + h)
        delta = jnp.where(here, jnp.sum(product, axis=1, keepdims=True), delta)
    out[:, :width] = q_ref[...]
    out[:, width : 2 * width] = do_ref[...]
    lse_pick = jnp.where((lse_column == lse_lane + dest * heads) & (lse_lane < heads), 1.0, 0.0)
    lse = dot_nn(lse_ref[...], lse_pick.astype(BF))
    delta_high = delta.astype(BF).astype(F32)
    stats = jnp.where(lane < heads, lse, jnp.where(lane < 2 * heads, delta_high, delta - delta_high))
    out[:, 2 * width : 2 * width + HEAD] = stats.astype(BF)


def pack_kernel(me_ref, q_ref, do_ref, o_ref, lse_ref, k_ref, v_ref, pk_ref, pv_ref, kv_out, *outs):
    parts = len(outs)
    width = q_ref.shape[1] // parts
    narrow = k_ref.shape[1] // parts
    start = 2 * width + HEAD
    me = me_ref[0]
    kv_out[:, :narrow] = pk_ref[...]
    kv_out[:, narrow:] = pv_ref[...]
    for k, out in enumerate(outs):
        dest = me ^ k
        wide = pl.ds(pl.multiple_of(dest * width, HEAD), width)
        thin = pl.ds(pl.multiple_of(dest * narrow, HEAD), narrow)
        pack_rows(
            dest, width // HEAD, q_ref.at[:, wide], do_ref.at[:, wide], o_ref.at[:, wide], lse_ref, out
        )
        out[:, start : start + narrow] = k_ref[:, thin]
        out[:, start + narrow :] = v_ref[:, thin]


def prompt_kernel(members, me_ref, q_ref, do_ref, o_ref, lse_ref, roll_ref, *rest):
    kv_refs, (dq_ref, part_ref, roll_dq_ref) = rest[:-3], rest[-3:]
    slots = len(kv_refs)
    rows = q_ref.shape[0]
    half = rows // 2
    narrow = kv_refs[0].shape[1] // 2
    groups = narrow // HEAD
    heads = lse_ref.shape[0]
    width = q_ref.shape[1]
    me = me_ref[0]
    count = members * half
    ones = jnp.ones((8, HEAD), BF)
    chunk_slots = max(1, min(slots, KEY_CHUNK // half))
    chunk = chunk_slots * half
    key_row = lax.broadcasted_iota(jnp.int32, (chunk, 1), 0)
    query_row = lax.broadcasted_iota(jnp.int32, (1, count), 1) % half
    stat_lane = lax.broadcasted_iota(jnp.int32, (half, HEAD), 1)
    spread = (
        lax.broadcasted_iota(jnp.int32, (heads, HEAD), 0) == lax.broadcasted_iota(jnp.int32, (heads, HEAD), 1)
    )
    all_lse = dot_tn(lse_ref[...], jnp.where(spread, 1.0, 0.0).astype(BF))
    for g in range(groups):
        queries, grads, lse_rows, delta_rows = [], [], [], []
        for s in range(2):
            low, high = s * half, (s + 1) * half
            queries.append(stacked_heads(q_ref, low, high, 0, g, members))
            grads.append(stacked_heads(do_ref, low, high, 0, g, members))
            outs = stacked_heads(o_ref, low, high, 0, g, members)
            up, down = split_sum(grads[s].astype(F32) * outs.astype(F32))
            delta_rows.append((dot_nt(ones, up) + dot_nt(ones, down))[0:1])
            lse = all_lse[low:high]
            picked = jnp.concatenate(
                [jnp.where(stat_lane == g * members + h, lse, 0.0) for h in range(members)], axis=0
            )
            lse_rows.append(dot_nt(ones, picked.astype(BF))[0:1] * LOG2E)
        queries.append(stacked_heads(roll_ref, 0, roll_ref.shape[0], 0, g, members))
        grads.append(stacked_heads(roll_ref, 0, roll_ref.shape[0], width, g, members))
        lse_row, delta_row = stat_rows([roll_ref], g, members, heads, width)
        lse_rows.append(lse_row)
        delta_rows.append(delta_row)
        grad_queries = [None, None, None]
        for side in range(2):
            for c in range(slots // chunk_slots):
                owned = kv_refs[c * chunk_slots : (c + 1) * chunk_slots]
                span = slice(side * half, (side + 1) * half)
                keys = jnp.concatenate([r[span, g * HEAD : (g + 1) * HEAD] for r in owned], axis=0)
                values = jnp.concatenate(
                    [r[span, narrow + g * HEAD : narrow + (g + 1) * HEAD] for r in owned], axis=0
                )
                owner = me ^ (c * chunk_slots + key_row // half)
                offset = key_row % half
                grad_key = grad_value = None
                for s in (1, 0, 2) if side == 0 else (1, 2):
                    mask = None
                    if s == side:
                        ahead = owner - me if side == 0 else me - owner
                        mask = ahead * half + offset <= query_row
                    dq, dk, dv = tile_grads(
                        keys, values, queries[s], grads[s], lse_rows[s], delta_rows[s], mask
                    )
                    grad_queries[s] = dq if grad_queries[s] is None else grad_queries[s] + dq
                    grad_key = dk if grad_key is None else grad_key + dk
                    grad_value = dv if grad_value is None else grad_value + dv
                grad_key = grad_key * SCALE
                for t in range(chunk_slots):
                    piece = slice(t * half, (t + 1) * half)
                    slot = c * chunk_slots + t
                    for total, at in ((grad_key, g * HEAD), (grad_value, narrow + g * HEAD)):
                        cols = slice(at, at + HEAD)
                        part_ref[slot, span, cols] = total[piece]
        for s in range(2):
            result = (grad_queries[s] * SCALE).T.astype(BF)
            for h in range(members):
                first = (g * members + h) * HEAD
                dq_ref[s * half : (s + 1) * half, first : first + HEAD] = result[h * half : (h + 1) * half]
        roll_dq_ref[g] = grad_queries[2]


def roll_kernel(parts, slots, members, me_ref, *rest):
    packs, rest = by_partner(rest[:parts], send_order(parts)), rest[parts:]
    kv_refs, rest = rest[:slots], rest[slots:]
    part_ref, roll_dq_ref, even_ref, odd_ref = rest[:4]
    backs = rest[4:]
    me = me_ref[0]
    rows = packs[0].shape[0]
    kv_rows = kv_refs[0].shape[0]
    narrow = kv_refs[0].shape[1] // 2
    groups = narrow // HEAD
    heads = groups * members
    width = heads * HEAD
    block = members * rows
    count = parts * block
    chunk_slots = max(1, min(slots, KEY_CHUNK // kv_rows))
    own_key = lax.broadcasted_iota(jnp.int32, (parts * rows, 1), 0)
    own_key_pos = (me ^ (own_key // rows)) * rows + own_key % rows
    own_query = lax.broadcasted_iota(jnp.int32, (1, count), 1)
    own_query_pos = (me ^ (own_query // block)) * rows + own_query % rows
    for g in range(groups):
        queries = jnp.concatenate([stacked_heads(p, 0, rows, 0, g, members) for p in packs], axis=0)
        grads = jnp.concatenate([stacked_heads(p, 0, rows, width, g, members) for p in packs], axis=0)
        lse_row, delta_row = stat_rows(packs, g, members, heads, width)
        first = 2 * width + HEAD + g * HEAD
        own_keys = jnp.concatenate([p[:, first : first + HEAD] for p in packs], axis=0)
        own_values = jnp.concatenate([p[:, first + narrow : first + narrow + HEAD] for p in packs], axis=0)
        grad_query, own_dk, own_dv = tile_grads(
            own_keys, own_values, queries, grads, lse_row, delta_row, own_key_pos <= own_query_pos
        )
        own_dk = (own_dk * SCALE).astype(BF)
        own_dv = own_dv.astype(BF)
        for k, back in enumerate(backs):
            piece = slice(k * rows, (k + 1) * rows)
            back[:, width + g * HEAD : width + (g + 1) * HEAD] = own_dk[piece]
            back[:, width + narrow + g * HEAD : width + narrow + (g + 1) * HEAD] = own_dv[piece]
        own_grad = grad_query[:, :block] + roll_dq_ref[g]
        others = slice(block, count)
        other_grad = grad_query[:, others]
        for c in range(slots // chunk_slots):
            owned = kv_refs[c * chunk_slots : (c + 1) * chunk_slots]
            keys = jnp.concatenate([r[:, g * HEAD : (g + 1) * HEAD] for r in owned], axis=0)
            values = jnp.concatenate(
                [r[:, narrow + g * HEAD : narrow + (g + 1) * HEAD] for r in owned], axis=0
            )
            dq, grad_key, grad_value = tile_grads(
                keys, values, queries[others], grads[others], lse_row[:, others], delta_row[:, others], None
            )
            other_grad = other_grad + dq
            grad_key = grad_key * SCALE
            for t in range(chunk_slots):
                slot = c * chunk_slots + t
                piece = slice(t * kv_rows, (t + 1) * kv_rows)
                for total, base in ((grad_key, 0), (grad_value, narrow)):
                    cols = slice(base + g * HEAD, base + (g + 1) * HEAD)
                    value = total[piece] + part_ref[slot, :, cols]
                    if slot % 2 == 0:
                        even_ref[slot // 2, :, cols] = value
                    else:
                        odd_ref[slot // 2, :, cols] = value.astype(BF)
        result = jnp.concatenate([(r * SCALE).T.astype(BF) for r in (own_grad, other_grad)], axis=0)
        for k, back in enumerate(backs):
            for h in range(members):
                start = k * block + h * rows
                first = (g * members + h) * HEAD
                back[:, first : first + HEAD] = result[start : start + rows]


def unpack_kernel(sums, me_ref, *rest):
    (own_ref, *got), rest = rest[:sums], rest[sums:]
    backs, (pk_ref, pv_ref, rq_ref, rk_ref, rv_ref) = by_partner(rest[:-5], return_order(len(rest) - 5)), rest[-5:]
    total = own_ref[...]
    for ref in got:
        total = total + ref[...].astype(F32)
    pk_ref[...] = total[:, : pk_ref.shape[1]].astype(BF)
    pv_ref[...] = total[:, pk_ref.shape[1] :].astype(BF)
    me = me_ref[0]
    width = rq_ref.shape[1] // len(backs)
    narrow = rk_ref.shape[1] // len(backs)
    for k, back in enumerate(backs):
        dest = me ^ k
        rq_ref[:, pl.ds(pl.multiple_of(dest * width, HEAD), width)] = back[:, :width]
        thin = pl.ds(pl.multiple_of(dest * narrow, HEAD), narrow)
        rk_ref[:, thin] = back[:, width : width + narrow]
        rv_ref[:, thin] = back[:, width + narrow :]


VMEM = pl.BlockSpec(memory_space=pltpu.VMEM)
SMEM = pl.BlockSpec(memory_space=pltpu.SMEM)


def call(kernel, name, outs, args, scalar=True, unread=0):
    return pl.pallas_call(
        kernel,
        name=name,
        out_shape=outs,
        in_specs=[SMEM] * scalar
        + [VMEM] * (len(args) - scalar - unread)
        + [pl.BlockSpec(memory_space=pl.ANY)] * unread,
        out_specs=[VMEM] * len(outs),
        compiler_params=pltpu.CompilerParams(vmem_limit_bytes=VMEM_LIMIT),
        cost_estimate=pl.CostEstimate(flops=0, bytes_accessed=0, transcendentals=0),
    )(*args)


def shape(dims, dtype):
    return jax.ShapeDtypeStruct(dims, dtype)


def vmem_shape(dims, dtype):
    return pltpu.VMEM(dims, dtype)


def swap(x, axis, k):
    n = lax.axis_size(axis)
    return lax.ppermute(x, axis, [(i, i ^ k) for i in range(n)])


def in_hbm(x):
    return pltpu.with_memory_space_constraint(x, pltpu.HBM)


def in_vmem(x):
    return pltpu.with_memory_space_constraint(x, pltpu.VMEM)


def on_device(
    prompt_query,
    prompt_key_rows,
    prompt_value_rows,
    prompt_dout,
    prompt_out,
    prompt_lse,
    roll_query,
    rollout_key_rows,
    rollout_value_rows,
    roll_dout,
    roll_out,
    roll_lse,
):
    slots = lax.axis_size("ctx")
    parts = lax.axis_size("roll")
    ctx_id = lax.axis_index("ctx").astype(jnp.int32).reshape(1)
    roll_id = lax.axis_index("roll").astype(jnp.int32).reshape(1)
    prompt_rows, width = prompt_query.shape
    narrow = prompt_key_rows.shape[1]
    members = width // narrow
    heads = width // HEAD
    rows = roll_query.shape[0]
    packed = 2 * width + HEAD + 2 * narrow

    kv, *packs = call(
        pack_kernel,
        "pack",
        [vmem_shape((prompt_rows, 2 * narrow), BF)] + [vmem_shape((rows, packed), BF)] * parts,
        (
            roll_id,
            *map(
                in_hbm,
                (
                    roll_query,
                    roll_dout,
                    roll_out,
                    roll_lse,
                    rollout_key_rows,
                    rollout_value_rows,
                    prompt_key_rows,
                    prompt_value_rows,
                ),
            ),
        ),
    )
    got = [swap(x, "roll", k) if k else x for k, x in enumerate(packs)]
    blocks = [kv]
    for s in range(1, slots):
        double = s % 2 and bin(s).count("1") > 2
        blocks.append(swap(blocks[s - 1], "ctx", 1) if double else swap(kv, "ctx", s))
    blocks = [in_vmem(x) for x in blocks]

    prompt_dq, part, roll_own_dq = call(
        functools.partial(prompt_kernel, members),
        "prompt_grads",
        [
            shape((prompt_rows, width), BF),
            vmem_shape((slots, prompt_rows, 2 * narrow), F32),
            vmem_shape((narrow // HEAD, HEAD, members * rows), F32),
        ],
        (ctx_id, *map(in_hbm, (prompt_query, prompt_dout, prompt_out, prompt_lse.T)), in_vmem(packs[0]), *blocks),
    )
    even, odd, *backs = call(
        functools.partial(roll_kernel, parts, slots, members),
        "roll_grads",
        [
            vmem_shape((slots // 2, prompt_rows, 2 * narrow), F32),
            vmem_shape((slots // 2, prompt_rows, 2 * narrow), BF),
        ]
        + [vmem_shape((rows, width + 2 * narrow), BF)] * parts,
        (roll_id, *[in_vmem(got[k]) for k in send_order(parts)], *blocks, in_vmem(part), in_vmem(roll_own_dq)),
    )
    odd_got = swap(odd, "ctx", 1)
    backs = [in_vmem(swap(x, "roll", k) if k else x) for k, x in enumerate(backs)]
    pair = [even[t] + odd_got[t].astype(F32) for t in range(slots // 2)]
    sums = [pair[0]] + [swap(pair[t].astype(BF), "ctx", 2 * t) for t in range(slots // 2 - 1, 0, -1)]
    prompt_dk, prompt_dv, roll_dq, roll_dk, roll_dv = call(
        functools.partial(unpack_kernel, len(sums)),
        "unpack",
        [
            shape((prompt_rows, narrow), BF),
            shape((prompt_rows, narrow), BF),
            shape((rows, parts * width), BF),
            shape((rows, parts * narrow), BF),
            shape((rows, parts * narrow), BF),
        ],
        (roll_id, *map(in_vmem, sums), *[backs[k] for k in return_order(parts)]),
    )
    return prompt_dq, prompt_dk, prompt_dv, roll_dq, roll_dk, roll_dv


def solution(mesh):
    both = P(("ctx", "roll"), None)
    split = P("ctx", "roll")
    return jax.shard_map(
        on_device,
        mesh=mesh,
        in_specs=(split,) * 6 + (both,) * 6,
        out_specs=(split,) * 3 + (both,) * 3,
        check_vma=False,
    )
```
